32 devices in a mesh: replica: 8 (over y, x, core), shard: 4 (over z).
Axes of the slice: x: 2, y: 2, z: 4, core: 2. Of those that a mesh axis runs over, the one named last changes fastest.
Arguments:
- grads: bfloat16 [8, 4, 256, 8192], P('replica', 'shard'), may hold values from -1.25 to 1.25
- master: float32 [256, 8192], P('shard'), may hold values from -0.003 to 0.003
- moment_one: float32 [256, 8192], P('shard'), may hold values from -0.75 to 0.75
- moment_two: float32 [256, 8192], P('shard'), may hold values from 0.005 to 0.2
Outputs:
- master_out: float32 [256, 8192], P('shard')
- moment_one_out: float32 [256, 8192], P('shard')
- moment_two_out: float32 [256, 8192], P('shard')
- weights: bfloat16 [256, 8192], replicated
The draws below stay inside these ranges and needn't reach their ends.
All inputs are finite; a program needn't handle non-finite values.
Results may differ from the reference program's by a relative error of at most 0.012.
Values may be sent and summed in bfloat16 or wider, within the bound.
A program may use at most 64 MiB of HBM per device.

```python
import math
import jax
import jax.numpy as jnp
from jax import lax

D = 8192
ROWS = 256
STEP = 20
N_REPLICA = 8
N_SHARD = 4


def spiked(values, stream_key, source, target, parts, factor):
    def block_of(dim):
        return (jnp.arange(values.shape[dim]) // (values.shape[dim] // parts)).reshape((-1,) + (1,) * (values.ndim - 1 - dim))

    one_side = jax.random.permutation(stream_key, parts)[block_of(target)]
    far = (block_of(target) + parts // 2) % parts
    return jnp.where((block_of(source) == one_side) | (block_of(source) == far), factor * values, values)


def levels(rng, dims, pieces, least, largest):
    gain, own = 1.0, jax.random.fold_in(rng, 6)
    for position, blocks in pieces:
        heights = jnp.exp(jax.random.uniform(jax.random.fold_in(own, position), (blocks,), jnp.float32, least / len(pieces), largest / len(pieces)))
        gain = gain * jnp.repeat(heights, dims[position] // blocks).reshape([-1 if axis == position else 1 for axis in range(len(dims))])
    return gain


def gaussian(stream_key, extent, spread, reach, split=(), dtype=jnp.bfloat16):
    level = levels(stream_key, extent, split, -0.22, 0.18) if split else 1.0
    entries = jax.random.normal(stream_key, extent, jnp.float32) * spread * level
    return jnp.minimum(jnp.maximum(entries, -reach), reach).astype(dtype)


def bell_draw_with(key, extent, scale, limit, shards, heavy, dtype=jnp.bfloat16):
    result = scale * jax.random.normal(key, extent, jnp.float32)
    if shards:
        result = result * levels(key, extent, shards, -0.22, 0.18)
    return jnp.clip(spiked(result, jax.random.fold_in(key, 3), *heavy), -limit, limit).astype(dtype)


def setup_inputs(seed: int = 0) -> dict:
    streams_of = jax.random.split(jax.random.key(seed), 5)
    grads = bell_draw_with(streams_of[0], (N_REPLICA, N_SHARD, ROWS, D), 0.0625, 1.25, ((0, 8), (1, 4)), (1, 2, 4, 2.0))
    master = jnp.clip(jax.random.uniform(streams_of[1], (ROWS, D), jnp.float32, -0.003, 0.003) * levels(streams_of[1], (ROWS, D), ((0, 4),), -0.4, 0.0), -0.003, 0.003)
    moment_one = gaussian(streams_of[2], (ROWS, D), 0.05, 0.75, ((0, 4),), jnp.float32)
    moment_two = jnp.clip(jnp.exp(math.log(0.2) - 3.6888795 * jax.random.uniform(streams_of[3], (ROWS, D), jnp.float32) ** levels(streams_of[3], (ROWS, D), ((0, 4),), -0.2, 0.2)), 0.005, 0.2)
    return dict(grads=grads, master=master, moment_one=moment_one, moment_two=moment_two)


def adam_update(total, master, moment_one, moment_two):
    first = 0.9 * moment_one + 0.1 * total
    second = 0.95 * moment_two + 0.05 * total * total
    first_hat = first / (1.0 - 0.9 ** STEP)
    second_hat = second / (1.0 - 0.95 ** STEP)
    updated = master - 0.0003 * (first_hat / (jnp.sqrt(second_hat) + 1e-08) + 0.1 * master)
    return (updated, first, second)

def reference(grads, master, moment_one, moment_two):

    def add_replica(carry, block):
        return (carry + lax.optimization_barrier(jnp.sum(block.astype(jnp.float32), axis=0)), None)
    total, unused = lax.scan(add_replica, jnp.zeros((ROWS, D), jnp.float32), grads)
    updated, first, second = adam_update(total, master, moment_one, moment_two)
    return (updated, first, second, updated.astype(jnp.bfloat16))
```

```python
import functools

import jax
import jax.numpy as jnp
from jax import lax
from jax.experimental import pallas as pl
from jax.experimental.pallas import tpu as pltpu
from jax.sharding import PartitionSpec as P

STEP = 20
MESH = pl.DeviceIdType.MESH


def adam_update(total, master, moment_one, moment_two):
    first = 0.9 * moment_one + 0.1 * total
    second = 0.95 * moment_two + 0.05 * total * total
    first_hat = first / (1.0 - 0.9**STEP)
    second_hat = second / (1.0 - 0.95**STEP)
    updated = master - 0.0003 * (first_hat / (jnp.sqrt(second_hat) + 1e-08) + 0.1 * master)
    return (updated, first, second)


def aligned(offset, width):
    return pl.ds(pl.multiple_of(offset, width), width)


def over_tiles(rows, columns, body):
    width = min(columns, 1024)
    across = columns // width

    def step(index, carry):
        row = pl.multiple_of(index // across * 16, 16)
        body(pl.ds(row, 16), pl.multiple_of(index % across * width, width), width)
        return carry

    lax.fori_loop(0, rows // 16 * across, step, 0)


def kernel(replicas, shards, grads, master, moment_one, moment_two, total_out, weights_out, *scratch):
    stages = replicas.bit_length() - 2
    own, theirs, from_shard, held, old_master, old_one, old_two = scratch[:7]
    arrived = scratch[7 : 7 + stages]
    summed = scratch[7 + stages : 7 + 2 * stages]
    (
        load_sem, state_sem, store_sem, core_send, core_recv, halve_send, halve_recv, shard_send, shard_recv,
        spread_send, spread_recv, join_send, join_recv, pair_send, pair_recv,
    ) = scratch[7 + 2 * stages :]

    rows = master.shape[0]
    columns = master.shape[1]
    half = columns // 2
    stream = half // 2
    me = lax.axis_index("replica")
    at = lax.axis_index("shard")
    bit = [me // (1 << b) % 2 for b in range(stages + 1)]
    partner = [me + (1 - 2 * bit[b]) * (1 << b) for b in range(stages + 1)]
    forward = list(range(1, stages + 1))
    orders = (forward, forward[::-1])

    def width(stage):
        return stream >> (stage + 1)

    def base(q, stage):
        offset = q * stream
        for u in range(stage + 1):
            offset = offset + bit[orders[q][u]] * width(u)
        return offset

    def remote(src, dst, send_sem, recv_sem, replica, shard):
        copy = pltpu.make_async_remote_copy(
            src_ref=src, dst_ref=dst, send_sem=send_sem, recv_sem=recv_sem,
            device_id=(replica, shard), device_id_type=MESH,
        )
        copy.start()
        return copy

    sent = []
    local = []

    loads = []
    for i in range(shards):
        block = lax.rem(at + 1 + i, shards)
        copy = pltpu.make_async_copy(
            grads.at[0, 0, aligned(block * rows, rows), aligned(bit[0] * half, half)], own.at[i], load_sem.at[i]
        )
        copy.start()
        loads.append(copy)
    states = []
    for s, (source, target) in enumerate(((master, old_master), (moment_one, old_one), (moment_two, old_two))):
        for q in range(2):
            offset = bit[0] * half + base(q, stages - 1)
            copy = pltpu.make_async_copy(
                source.at[:, aligned(offset, width(stages - 1))], target.at[q], state_sem.at[s, q]
            )
            copy.start()
            states.append(copy)

    barrier = pltpu.get_barrier_semaphore()
    for other in partner:
        pl.semaphore_signal(barrier, inc=1, device_id=(other, at), device_id_type=MESH)
    for d in range(1, shards):
        pl.semaphore_signal(barrier, inc=1, device_id=(me, lax.rem(at + d, shards)), device_id_type=MESH)
    pl.semaphore_wait(barrier, len(partner) + shards - 1)

    core = []
    for i in range(shards):
        block = lax.rem(at + 1 + i, shards)
        core.append(
            remote(
                grads.at[0, 0, aligned(block * rows, rows), aligned((1 - bit[0]) * half, half)],
                theirs.at[i], core_send.at[i], core_recv.at[i], partner[0], at,
            )
        )
    sent += core
    halving = {}
    shard_copies = []

    def start_halving(i, stage):
        for q in range(2):
            wide = width(stage)
            b = orders[q][stage]
            if stage == 0:
                source = own.at[i, :, aligned(q * stream + (1 - bit[b]) * wide, wide)]
            else:
                source = summed[stage - 1].at[i, q, :, aligned((1 - bit[b]) * wide, wide)]
            halving[i, stage, q] = remote(
                source, arrived[stage].at[i, q], halve_send.at[i, stage, q], halve_recv.at[i, stage, q], partner[b], at
            )
            sent.append(halving[i, stage, q])

    def phase(i, step):
        if step == 0:
            loads[i].wait()
            core[i].wait_recv()

            def add(r, c, wide):
                mine = own[i, r, pl.ds(c, wide)].astype(jnp.float32)
                own[i, r, pl.ds(c, wide)] = (mine + theirs[i, r, pl.ds(c, wide)].astype(jnp.float32)).astype(jnp.bfloat16)

            over_tiles(rows, half, add)
            start_halving(i, 0)
            return
        stage = step - 1
        for q in range(2):
            halving[i, stage, q].wait_recv()
            kept = bit[orders[q][stage]] * width(stage)

            def add(r, c, wide):
                if stage == 0:
                    mine = own[i, r, pl.ds(pl.multiple_of(q * stream + kept + c, wide), wide)]
                else:
                    mine = summed[stage - 1][i, q, r, pl.ds(pl.multiple_of(kept + c, wide), wide)]
                other = arrived[stage][i, q, r, pl.ds(c, wide)]
                summed[stage][i, q, r, pl.ds(c, wide)] = (
                    mine.astype(jnp.float32) + other.astype(jnp.float32)
                ).astype(jnp.bfloat16)

            over_tiles(rows, width(stage), add)
        if step < stages:
            start_halving(i, step)
        elif i < shards - 1:
            copy = remote(
                summed[stages - 1].at[i], from_shard.at[i], shard_send.at[i], shard_recv.at[i],
                me, lax.rem(at + 1 + i, shards),
            )
            shard_copies.append(copy)
            sent.append(copy)

    for tick in range(shards + stages):
        for step in range(stages + 1):
            if 0 <= tick - step < shards:
                phase(tick - step, step)

    for copy in states:
        copy.wait()
    for copy in shard_copies:
        copy.wait_recv()
    piece = width(stages - 1)
    for q in range(2):
        offset = base(q, stages - 1)

        def update(r, c, wide):
            total = summed[stages - 1][shards - 1, q, r, pl.ds(c, wide)].astype(jnp.float32)
            for i in range(shards - 1):
                total = total + from_shard[i, q, r, pl.ds(c, wide)].astype(jnp.float32)
            rounded = total.astype(jnp.bfloat16)
            where = pl.ds(pl.multiple_of(offset + c, wide), wide)
            held[1, r, where] = rounded
            updated, _, _ = adam_update(
                rounded.astype(jnp.float32), old_master[q, r, pl.ds(c, wide)],
                old_one[q, r, pl.ds(c, wide)], old_two[q, r, pl.ds(c, wide)],
            )
            held[0, r, where] = updated.astype(jnp.bfloat16)

        over_tiles(rows, piece, update)

    spread = {}
    for d in range(1, shards):
        for q in range(2):
            where = aligned(base(q, stages - 1), piece)
            spread[d, q] = remote(
                held.at[0, :, where], held.at[1 + d, :, where], spread_send.at[d - 1, q], spread_recv.at[d - 1, q],
                me, lax.rem(at + d, shards),
            )
            sent.append(spread[d, q])
    joining = {}
    pairs = []

    def join(j, stage):
        for q in range(2):
            where = aligned(base(q, stage), width(stage))
            joining[j, stage, q] = remote(
                held.at[j, :, where], held.at[j, :, where], join_send.at[j, stage, q], join_recv.at[j, stage, q],
                partner[orders[q][stage]], at,
            )
            sent.append(joining[j, stage, q])

    def gather(j, step):
        if step == 0:
            if j > 1:
                for q in range(2):
                    spread[j - 1, q].wait_recv()
        else:
            for q in range(2):
                joining[j, stages - step, q].wait_recv()
        if step < stages:
            join(j, stages - 1 - step)
            return
        if j == 1:
            target = total_out.at[:, aligned(bit[0] * half, half)]
        else:
            block = at if j == 0 else lax.rem(at + shards - (j - 1), shards)
            target = weights_out.at[aligned(block * rows, rows), aligned(bit[0] * half, half)]
        pair = remote(held.at[j], target, pair_send.at[j], pair_recv.at[j], partner[0], at)
        pairs.append(pair)
        sent.append(pair)
        copy = pltpu.make_async_copy(held.at[j], target, store_sem.at[j])
        copy.start()
        local.append(copy)

    for tick in range(shards + 1 + stages):
        for step in range(stages + 1):
            if 0 <= tick - step < shards + 1:
                gather(tick - step, step)

    for copy in pairs:
        copy.wait_recv()
    for copy in local:
        copy.wait()
    for copy in sent:
        copy.wait_send()


def local(replicas, shards, grads, master, moment_one, moment_two):
    rows, columns = master.shape
    half = columns // 2
    stages = replicas.bit_length() - 2
    piece = half // 2 >> stages
    halves = [(shards, 2, rows, half // 2 >> (t + 1)) for t in range(stages)]
    sem = pltpu.SemaphoreType.DMA
    total, weights = pl.pallas_call(
        functools.partial(kernel, replicas, shards),
        out_shape=(
            jax.ShapeDtypeStruct((rows, columns), jnp.bfloat16),
            jax.ShapeDtypeStruct((rows * shards, columns), jnp.bfloat16),
        ),
        in_specs=[pl.BlockSpec(memory_space=pl.ANY)] * 4,
        out_specs=[pl.BlockSpec(memory_space=pl.ANY)] * 2,
        scratch_shapes=[
            pltpu.VMEM((shards, rows, half), jnp.bfloat16),
            pltpu.VMEM((shards, rows, half), jnp.bfloat16),
            pltpu.VMEM((shards - 1, 2, rows, piece), jnp.bfloat16),
            pltpu.VMEM((shards + 1, rows, half), jnp.bfloat16),
            *[pltpu.VMEM((2, rows, piece), jnp.float32)] * 3,
            *[pltpu.VMEM(shape, jnp.bfloat16) for shape in halves * 2],
            sem((shards,)),
            sem((3, 2)),
            sem((shards + 1,)),
            *[sem((shards,))] * 2,
            *[sem((shards, stages, 2))] * 2,
            *[sem((shards - 1,))] * 2,
            *[sem((shards - 1, 2))] * 2,
            *[sem((shards + 1, stages, 2))] * 2,
            *[sem((shards + 1,))] * 2,
        ],
        compiler_params=pltpu.CompilerParams(
            collective_id=0, has_side_effects=True, vmem_limit_bytes=24 * 1024 * 1024
        ),
        name="reduce_update_gather",
    )(grads, master, moment_one, moment_two)
    updated, first, second = adam_update(total.astype(jnp.float32), master, moment_one, moment_two)
    return (updated, first, second, weights)


def solution(mesh):
    placed = (
        P("replica", "shard", None, None),
        P("shard", None),
        P("shard", None),
        P("shard", None),
    )
    return jax.shard_map(
        functools.partial(local, mesh.shape["replica"], mesh.shape["shard"]),
        mesh=mesh,
        in_specs=placed,
        out_specs=(P("shard", None), P("shard", None), P("shard", None), P()),
        check_vma=False,
    )
```

```python
import functools

import jax
import jax.numpy as jnp
from jax import lax
from jax.experimental import pallas as pl
from jax.experimental.pallas import tpu as pltpu
from jax.sharding import PartitionSpec as P

STEP = 20
MESH = pl.DeviceIdType.MESH


def adam_update(total, master, moment_one, moment_two):
    first = 0.9 * moment_one + 0.1 * total
    second = 0.95 * moment_two + 0.05 * total * total
    first_hat = first / (1.0 - 0.9**STEP)
    second_hat = second / (1.0 - 0.95**STEP)
    updated = master - 0.0003 * (first_hat / (jnp.sqrt(second_hat) + 1e-08) + 0.1 * master)
    return (updated, first, second)


def aligned(offset, width):
    return pl.ds(pl.multiple_of(offset, width), width)


def over_tiles(rows, columns, body, widest=2048):
    width = min(columns, widest)
    across = columns // width

    def step(index, carry):
        row = pl.multiple_of(index // across * 16, 16)
        body(pl.ds(row, 16), pl.multiple_of(index % across * width, width), width)
        return carry

    lax.fori_loop(0, rows // 16 * across, step, 0)


def kernel(
    replicas, shards, grads, master, moment_one, moment_two,
    master_out, one_out, two_out, weights_out, *scratch,
):
    stages = replicas.bit_length() - 2
    (
        own, theirs, from_shard, held, total_pair, own_weights, row_weights, all_master, all_one, all_two,
    ) = scratch[:10]
    arrived = scratch[10 : 10 + stages]
    summed = scratch[10 + stages : 10 + 2 * stages]
    (
        load_sem, state_sem, store_sem, out_sem, core_send, core_recv, halve_send, halve_recv, shard_send, shard_recv,
        spread_send, spread_recv, join_send, join_recv, pair_send, pair_recv,
    ) = scratch[10 + 2 * stages :]

    rows = master.shape[0]
    columns = master.shape[1]
    half = columns // 2
    stream = half // 2
    me = lax.axis_index("replica")
    at = lax.axis_index("shard")
    bit = [me // (1 << b) % 2 for b in range(stages + 1)]
    partner = [me + (1 - 2 * bit[b]) * (1 << b) for b in range(stages + 1)]
    forward = list(range(1, stages + 1))
    orders = (forward, forward[::-1])

    def width(stage):
        return stream >> (stage + 1)

    def base(q, stage):
        offset = q * stream
        for u in range(stage + 1):
            offset = offset + bit[orders[q][u]] * width(u)
        return offset

    def remote(src, dst, send_sem, recv_sem, replica, shard):
        copy = pltpu.make_async_remote_copy(
            src_ref=src, dst_ref=dst, send_sem=send_sem, recv_sem=recv_sem,
            device_id=(replica, shard), device_id_type=MESH,
        )
        copy.start()
        return copy

    sent = []
    local = []

    loads = []
    for i in range(shards):
        block = lax.rem(at + 1 + i, shards)
        copy = pltpu.make_async_copy(
            grads.at[0, 0, aligned(block * rows, rows), aligned(bit[0] * half, half)], own.at[i], load_sem.at[i]
        )
        copy.start()
        loads.append(copy)
    barrier = pltpu.get_barrier_semaphore()
    for other in partner:
        pl.semaphore_signal(barrier, inc=1, device_id=(other, at), device_id_type=MESH)
    for d in range(1, shards):
        pl.semaphore_signal(barrier, inc=1, device_id=(me, lax.rem(at + d, shards)), device_id_type=MESH)
    pl.semaphore_wait(barrier, len(partner) + shards - 1)

    core = []

    def start_core(i):
        block = lax.rem(at + 1 + i, shards)
        core.append(
            remote(
                grads.at[0, 0, aligned(block * rows, rows), aligned((1 - bit[0]) * half, half)],
                theirs.at[i], core_send.at[i], core_recv.at[i], partner[0], at,
            )
        )
        sent.append(core[i])

    for i in range(2):
        start_core(i)
    states = []
    for s, (source, target) in enumerate(((master, all_master), (moment_one, all_one), (moment_two, all_two))):
        copy = pltpu.make_async_copy(source, target, state_sem.at[s])
        copy.start()
        states.append(copy)
    halving = {}
    shard_copies = []

    def start_halving(i, stage, q):
        wide = width(stage)
        b = orders[q][stage]
        if stage == 0:
            source = own.at[i, :, aligned(q * stream + (1 - bit[b]) * wide, wide)]
        else:
            source = summed[stage - 1].at[i, q, :, aligned((1 - bit[b]) * wide, wide)]
        halving[i, stage, q] = remote(
            source, arrived[stage].at[i, q], halve_send.at[i, stage, q], halve_recv.at[i, stage, q], partner[b], at
        )
        sent.append(halving[i, stage, q])

    def phase(i, step):
        if step == 0:
            loads[i].wait()
            core[i].wait_recv()
            if i + 2 < shards:
                start_core(i + 2)
            for q in range(2):

                def add(r, c, wide):
                    where = pl.ds(pl.multiple_of(q * stream + c, wide), wide)
                    own[i, r, where] = own[i, r, where] + theirs[i, r, where]

                over_tiles(rows, stream, add)
                start_halving(i, 0, q)
            return
        stage = step - 1
        for q in range(2):
            halving[i, stage, q].wait_recv()
            kept = bit[orders[q][stage]] * width(stage)

            def add(r, c, wide):
                if stage == 0:
                    mine = own[i, r, pl.ds(pl.multiple_of(q * stream + kept + c, wide), wide)]
                else:
                    mine = summed[stage - 1][i, q, r, pl.ds(pl.multiple_of(kept + c, wide), wide)]
                summed[stage][i, q, r, pl.ds(c, wide)] = mine + arrived[stage][i, q, r, pl.ds(c, wide)]

            over_tiles(rows, width(stage), add)
            if step < stages:
                start_halving(i, step, q)
        if step == stages and i < shards - 1:
            copy = remote(
                summed[stages - 1].at[i], from_shard.at[i], shard_send.at[i], shard_recv.at[i],
                me, lax.rem(at + 1 + i, shards),
            )
            shard_copies.append(copy)
            sent.append(copy)

    for tick in range(shards + stages):
        for step in range(stages + 1):
            if 0 <= tick - step < shards:
                phase(tick - step, step)

    for copy in states:
        copy.wait()
    for copy in shard_copies:
        copy.wait_recv()
    piece = width(stages - 1)
    for q in range(2):
        offset = base(q, stages - 1)

        def finish(r, c, wide):
            total = summed[stages - 1][shards - 1, q, r, pl.ds(c, wide)].astype(jnp.float32)
            for i in range(shards - 1):
                total = total + from_shard[i, q, r, pl.ds(c, wide)].astype(jnp.float32)
            rounded = total.astype(jnp.bfloat16)
            held[0, r, pl.ds(pl.multiple_of(offset + c, wide), wide)] = rounded
            where = pl.ds(pl.multiple_of(bit[0] * half + offset + c, wide), wide)
            updated, _, _ = adam_update(
                rounded.astype(jnp.float32), all_master[r, where], all_one[r, where], all_two[r, where]
            )
            own_weights[q, r, pl.ds(c, wide)] = updated.astype(jnp.bfloat16)

        over_tiles(rows, piece, finish, 512)

    spread = {}
    for d in range(1, shards):
        for q in range(2):
            spread[d, q] = remote(
                own_weights.at[q], held.at[d, :, aligned(base(q, stages - 1), piece)],
                spread_send.at[d - 1, q], spread_recv.at[d - 1, q], me, lax.rem(at + d, shards),
            )
            sent.append(spread[d, q])
    joining = {}
    pairs = []
    todo = []

    def join(j, stage, q):
        where = aligned(base(q, stage), width(stage))
        joining[j, stage, q] = remote(
            held.at[j, :, where], held.at[j, :, where], join_send.at[j, stage, q], join_recv.at[j, stage, q],
            partner[orders[q][stage]], at,
        )
        sent.append(joining[j, stage, q])

    def update_rows(side, group):
        start = (bit[0] if side == 0 else 1 - bit[0]) * half
        if side == 1 and group == 0:
            pairs[0].wait_recv()

        def update(r, c, wide):
            r = pl.ds(group * 16, 16)
            total = held[0, r, pl.ds(c, wide)] if side == 0 else total_pair[r, pl.ds(c, wide)]
            where = pl.ds(pl.multiple_of(start + c, wide), wide)
            updated, first, second = adam_update(
                total.astype(jnp.float32), all_master[r, where], all_one[r, where], all_two[r, where]
            )
            all_master[r, where] = updated
            all_one[r, where] = first
            all_two[r, where] = second
            row_weights[r, where] = updated.astype(jnp.bfloat16)

        over_tiles(16, half, update, 512)
        if group == rows // 16 - 1:
            where = aligned(start, half)
            targets = (
                (all_master, master_out.at[:, where]),
                (all_one, one_out.at[:, where]),
                (all_two, two_out.at[:, where]),
                (row_weights, weights_out.at[aligned(at * rows, rows), where]),
            )
            for s, (source, target) in enumerate(targets):
                copy = pltpu.make_async_copy(source.at[:, where], target, out_sem.at[side, s])
                copy.start()
                local.append(copy)

    def gather(j, step):
        for q in range(2):
            if step > 0:
                joining[j, stages - step, q].wait_recv()
            elif j > 0:
                spread[j, q].wait_recv()
            if step < stages:
                join(j, stages - 1 - step, q)
        if step < stages:
            return
        if j == 0:
            pair = remote(held.at[0], total_pair, pair_send.at[0], pair_recv.at[0], partner[0], at)
            todo.extend((side, group) for side in range(2) for group in range(rows // 16))
        else:
            block = lax.rem(at + shards - j, shards)
            target = weights_out.at[aligned(block * rows, rows), aligned(bit[0] * half, half)]
            pair = remote(held.at[j], target, pair_send.at[j], pair_recv.at[j], partner[0], at)
            copy = pltpu.make_async_copy(held.at[j], target, store_sem.at[j - 1])
            copy.start()
            local.append(copy)
        pairs.append(pair)
        sent.append(pair)

    for tick in range(shards + stages):
        for step in range(stages + 1):
            if 0 <= tick - step < shards:
                gather(tick - step, step)
                if todo:
                    update_rows(*todo.pop(0))
    while todo:
        update_rows(*todo.pop(0))

    for copy in pairs[1:]:
        copy.wait_recv()
    for copy in local:
        copy.wait()
    for copy in sent:
        copy.wait_send()


def write_out(*refs):
    count = len(refs) // 2
    copies = [pltpu.make_async_copy(refs[k], refs[count + k], refs[-1].at[k]) for k in range(count)]
    for copy in copies:
        copy.start()
    for copy in copies:
        copy.wait()


def local(replicas, shards, grads, master, moment_one, moment_two):
    rows, columns = master.shape
    half = columns // 2
    stages = replicas.bit_length() - 2
    piece = half // 2 >> stages
    halves = [(shards, 2, rows, half // 2 >> (t + 1)) for t in range(stages)]
    sem = pltpu.SemaphoreType.DMA
    hbm = pl.BlockSpec(memory_space=pltpu.HBM)
    outs = tuple(
        jax.ShapeDtypeStruct(shape, dtype)
        for shape, dtype in [((rows, columns), jnp.float32)] * 3 + [((rows * shards, columns), jnp.bfloat16)]
    )
    results = pl.pallas_call(
        functools.partial(kernel, replicas, shards),
        out_shape=outs,
        in_specs=[hbm] * 4,
        out_specs=[pl.BlockSpec(memory_space=pl.ANY)] * 4,
        scratch_shapes=[
            pltpu.VMEM((shards, rows, half), jnp.bfloat16),
            pltpu.VMEM((shards, rows, half), jnp.bfloat16),
            pltpu.VMEM((shards - 1, 2, rows, piece), jnp.bfloat16),
            pltpu.VMEM((shards, rows, half), jnp.bfloat16),
            pltpu.VMEM((rows, half), jnp.bfloat16),
            pltpu.VMEM((2, rows, piece), jnp.bfloat16),
            pltpu.VMEM((rows, columns), jnp.bfloat16),
            *[pltpu.VMEM((rows, columns), jnp.float32)] * 3,
            *[pltpu.VMEM(shape, jnp.bfloat16) for shape in halves * 2],
            sem((shards,)),
            sem((3,)),
            sem((shards - 1,)),
            sem((2, 4)),
            *[sem((shards,))] * 2,
            *[sem((shards, stages, 2))] * 2,
            *[sem((shards - 1,))] * 2,
            *[sem((shards - 1, 2))] * 2,
            *[sem((shards, stages, 2))] * 2,
            *[sem((shards,))] * 2,
        ],
        compiler_params=pltpu.CompilerParams(
            collective_id=0, has_side_effects=True, vmem_limit_bytes=28 * 1024 * 1024
        ),
        name="reduce_update_gather",
    )(*(pltpu.with_memory_space_constraint(x, pltpu.HBM) for x in (grads, master, moment_one, moment_two)))
    return pl.pallas_call(
        write_out,
        out_shape=outs,
        in_specs=[pl.BlockSpec(memory_space=pl.ANY)] * 4,
        out_specs=[hbm] * 4,
        scratch_shapes=[sem((4,))],
        name="write_out",
    )(*results)


def solution(mesh):
    placed = (
        P("replica", "shard", None, None),
        P("shard", None),
        P("shard", None),
        P("shard", None),
    )
    return jax.shard_map(
        functools.partial(local, mesh.shape["replica"], mesh.shape["shard"]),
        mesh=mesh,
        in_specs=placed,
        out_specs=(P("shard", None), P("shard", None), P("shard", None), P()),
        check_vma=False,
    )
```

```python
import functools

import jax
import jax.numpy as jnp
from jax import lax
from jax.experimental import pallas as pl
from jax.experimental.pallas import tpu as pltpu
from jax.sharding import PartitionSpec as P

STEP = 20
MESH = pl.DeviceIdType.MESH


def adam_update(total, master, moment_one, moment_two):
    first = 0.9 * moment_one + 0.1 * total
    second = 0.95 * moment_two + 0.05 * total * total
    first_hat = first / (1.0 - 0.9**STEP)
    second_hat = second / (1.0 - 0.95**STEP)
    updated = master - 0.0003 * (first_hat / (jnp.sqrt(second_hat) + 1e-08) + 0.1 * master)
    return (updated, first, second)


def aligned(offset, width):
    return pl.ds(pl.multiple_of(offset, width), width)


def over_tiles(rows, columns, body, widest=2048):
    width = min(columns, widest)
    across = columns // width

    def step(index, carry):
        row = pl.multiple_of(index // across * 16, 16)
        body(pl.ds(row, 16), pl.multiple_of(index % across * width, width), width)
        return carry

    lax.fori_loop(0, rows // 16 * across, step, 0)


def kernel(
    replicas, shards, grads, master, moment_one, moment_two,
    master_out, one_out, two_out, weights_out, *scratch,
):
    stages = replicas.bit_length() - 2
    (
        own, theirs, from_shard, held, total_pair, own_weights, row_weights, all_master, all_one, all_two,
    ) = scratch[:10]
    arrived = scratch[10 : 10 + stages]
    summed = scratch[10 + stages : 10 + 2 * stages]
    (
        load_sem, state_sem, store_sem, out_sem, core_send, core_recv, halve_send, halve_recv, shard_send, shard_recv,
        spread_send, spread_recv, join_send, join_recv, pair_send, pair_recv,
    ) = scratch[10 + 2 * stages :]

    rows = master.shape[0]
    columns = master.shape[1]
    half = columns // 2
    stream = half // 2
    me = lax.axis_index("replica")
    at = lax.axis_index("shard")
    bit = [me // (1 << b) % 2 for b in range(stages + 1)]
    partner = [me + (1 - 2 * bit[b]) * (1 << b) for b in range(stages + 1)]
    forward = list(range(1, stages + 1))
    orders = (forward, forward[::-1])

    def width(stage):
        return stream >> (stage + 1)

    def base(q, stage):
        offset = q * stream
        for u in range(stage + 1):
            offset = offset + bit[orders[q][u]] * width(u)
        return offset

    def remote(src, dst, send_sem, recv_sem, replica, shard):
        copy = pltpu.make_async_remote_copy(
            src_ref=src, dst_ref=dst, send_sem=send_sem, recv_sem=recv_sem,
            device_id=(replica, shard), device_id_type=MESH,
        )
        copy.start()
        return copy

    sent = []
    local = []

    loads = []
    for i in range(shards):
        block = lax.rem(at + 1 + i, shards)
        copy = pltpu.make_async_copy(
            grads.at[0, 0, aligned(block * rows, rows), aligned(bit[0] * half, half)], own.at[i], load_sem.at[i]
        )
        copy.start()
        loads.append(copy)
    barrier = pltpu.get_barrier_semaphore()
    for other in partner:
        pl.semaphore_signal(barrier, inc=1, device_id=(other, at), device_id_type=MESH)
    for d in range(1, shards):
        pl.semaphore_signal(barrier, inc=1, device_id=(me, lax.rem(at + d, shards)), device_id_type=MESH)
    pl.semaphore_wait(barrier, len(partner) + shards - 1)

    core = []

    def start_core(i):
        block = lax.rem(at + 1 + i, shards)
        core.append(
            remote(
                grads.at[0, 0, aligned(block * rows, rows), aligned((1 - bit[0]) * half, half)],
                theirs.at[i], core_send.at[i], core_recv.at[i], partner[0], at,
            )
        )
        sent.append(core[i])

    for i in range(2):
        start_core(i)
    states = []
    for s, (source, target) in enumerate(((master, all_master), (moment_one, all_one), (moment_two, all_two))):
        copy = pltpu.make_async_copy(source, target, state_sem.at[s])
        copy.start()
        states.append(copy)
    halving = {}
    shard_copies = []

    def start_halving(i, stage, q):
        wide = width(stage)
        b = orders[q][stage]
        if stage == 0:
            source = own.at[i, :, aligned(q * stream + (1 - bit[b]) * wide, wide)]
        else:
            source = summed[stage - 1].at[i, q, :, aligned((1 - bit[b]) * wide, wide)]
        halving[i, stage, q] = remote(
            source, arrived[stage].at[i, q], halve_send.at[i, stage, q], halve_recv.at[i, stage, q], partner[b], at
        )
        sent.append(halving[i, stage, q])

    def phase(i, step):
        if step == 0:
            loads[i].wait()
            core[i].wait_recv()
            if i + 2 < shards:
                start_core(i + 2)
            for q in range(2):

                def add(r, c, wide):
                    where = pl.ds(pl.multiple_of(q * stream + c, wide), wide)
                    own[i, r, where] = own[i, r, where] + theirs[i, r, where]

                over_tiles(rows, stream, add)
                start_halving(i, 0, q)
            return
        stage = step - 1
        for q in range(2):
            halving[i, stage, q].wait_recv()
            kept = bit[orders[q][stage]] * width(stage)

            def add(r, c, wide):
                if stage == 0:
                    mine = own[i, r, pl.ds(pl.multiple_of(q * stream + kept + c, wide), wide)]
                else:
                    mine = summed[stage - 1][i, q, r, pl.ds(pl.multiple_of(kept + c, wide), wide)]
                summed[stage][i, q, r, pl.ds(c, wide)] = mine + arrived[stage][i, q, r, pl.ds(c, wide)]

            over_tiles(rows, width(stage), add)
            if step < stages:
                start_halving(i, step, q)
        if step == stages and i < shards - 1:
            copy = remote(
                summed[stages - 1].at[i], from_shard.at[i], shard_send.at[i], shard_recv.at[i],
                me, lax.rem(at + 1 + i, shards),
            )
            shard_copies.append(copy)
            sent.append(copy)

    for tick in range(shards + stages):
        for step in range(stages + 1):
            if 0 <= tick - step < shards:
                phase(tick - step, step)

    for copy in shard_copies:
        copy.wait_recv()
    piece = width(stages - 1)
    joining = {}
    pairs = []
    todo = []

    def join(j, stage, q):
        where = aligned(base(q, stage), width(stage))
        joining[j, stage, q] = remote(
            held.at[j, :, where], held.at[j, :, where], join_send.at[j, stage, q], join_recv.at[j, stage, q],
            partner[orders[q][stage]], at,
        )
        sent.append(joining[j, stage, q])

    for q in range(2):
        offset = base(q, stages - 1)

        def finish(r, c, wide):
            total = summed[stages - 1][shards - 1, q, r, pl.ds(c, wide)].astype(jnp.float32)
            for i in range(shards - 1):
                total = total + from_shard[i, q, r, pl.ds(c, wide)].astype(jnp.float32)
            held[0, r, pl.ds(pl.multiple_of(offset + c, wide), wide)] = total.astype(jnp.bfloat16)

        over_tiles(rows, piece, finish, 512)
        join(0, stages - 1, q)

    for copy in states:
        copy.wait()
    for q in range(2):
        offset = base(q, stages - 1)

        def own_update(r, c, wide):
            total = held[0, r, pl.ds(pl.multiple_of(offset + c, wide), wide)].astype(jnp.float32)
            where = pl.ds(pl.multiple_of(bit[0] * half + offset + c, wide), wide)
            updated, _, _ = adam_update(total, all_master[r, where], all_one[r, where], all_two[r, where])
            own_weights[q, r, pl.ds(c, wide)] = updated.astype(jnp.bfloat16)

        over_tiles(rows, piece, own_update, 512)

    spread = {}

    def start_spread(d):
        for q in range(2):
            spread[d, q] = remote(
                own_weights.at[q], held.at[d, :, aligned(base(q, stages - 1), piece)],
                spread_send.at[d - 1, q], spread_recv.at[d - 1, q], me, lax.rem(at + d, shards),
            )
            sent.append(spread[d, q])

    def update_rows(side, group):
        start = (bit[0] if side == 0 else 1 - bit[0]) * half
        if side == 1 and group == 0:
            pairs[0].wait_recv()

        def update(r, c, wide):
            r = pl.ds(group * 16, 16)
            total = held[0, r, pl.ds(c, wide)] if side == 0 else total_pair[r, pl.ds(c, wide)]
            where = pl.ds(pl.multiple_of(start + c, wide), wide)
            updated, first, second = adam_update(
                total.astype(jnp.float32), all_master[r, where], all_one[r, where], all_two[r, where]
            )
            all_master[r, where] = updated
            all_one[r, where] = first
            all_two[r, where] = second
            row_weights[r, where] = updated.astype(jnp.bfloat16)

        over_tiles(16, half, update, 512)
        if group == rows // 16 - 1:
            where = aligned(start, half)
            targets = (
                (all_master, master_out.at[:, where]),
                (all_one, one_out.at[:, where]),
                (all_two, two_out.at[:, where]),
                (row_weights, weights_out.at[aligned(at * rows, rows), where]),
            )
            for s, (source, target) in enumerate(targets):
                copy = pltpu.make_async_copy(source.at[:, where], target, out_sem.at[side, s])
                copy.start()
                local.append(copy)

    def gather(j, step):
        for q in range(2):
            if step > 0:
                joining[j, stages - step, q].wait_recv()
            elif j > 0:
                spread[j, q].wait_recv()
            if step < stages and (j, step) != (0, 0):
                join(j, stages - 1 - step, q)
        if step < stages:
            return
        if j == 0:
            pair = remote(held.at[0], total_pair, pair_send.at[0], pair_recv.at[0], partner[0], at)
            todo.extend((side, group) for side in range(2) for group in range(rows // 16))
        else:
            block = lax.rem(at + shards - j, shards)
            target = weights_out.at[aligned(block * rows, rows), aligned(bit[0] * half, half)]
            pair = remote(held.at[j], target, pair_send.at[j], pair_recv.at[j], partner[0], at)
            copy = pltpu.make_async_copy(held.at[j], target, store_sem.at[j - 1])
            copy.start()
            local.append(copy)
        pairs.append(pair)
        sent.append(pair)

    for tick in range(shards + stages):
        steps = [step for step in reversed(range(stages + 1)) if 0 <= tick - step < shards]
        for place, step in enumerate(steps):
            gather(tick - step, step)
            if place == 0 and tick + 1 < shards:
                start_spread(tick + 1)
            if todo:
                update_rows(*todo.pop(0))
    while todo:
        update_rows(*todo.pop(0))

    for copy in pairs[1:]:
        copy.wait_recv()
    for copy in local:
        copy.wait()
    for copy in sent:
        copy.wait_send()


def write_out(*refs):
    count = len(refs) // 2
    copies = [pltpu.make_async_copy(refs[k], refs[count + k], refs[-1].at[k]) for k in range(count)]
    for copy in copies:
        copy.start()
    for copy in copies:
        copy.wait()


def local(replicas, shards, grads, master, moment_one, moment_two):
    rows, columns = master.shape
    half = columns // 2
    stages = replicas.bit_length() - 2
    piece = half // 2 >> stages
    halves = [(shards, 2, rows, half // 2 >> (t + 1)) for t in range(stages)]
    sem = pltpu.SemaphoreType.DMA
    hbm = pl.BlockSpec(memory_space=pltpu.HBM)
    outs = tuple(
        jax.ShapeDtypeStruct(shape, dtype)
        for shape, dtype in [((rows, columns), jnp.float32)] * 3 + [((rows * shards, columns), jnp.bfloat16)]
    )
    results = pl.pallas_call(
        functools.partial(kernel, replicas, shards),
        out_shape=outs,
        in_specs=[hbm] * 4,
        out_specs=[pl.BlockSpec(memory_space=pl.ANY)] * 4,
        scratch_shapes=[
            pltpu.VMEM((shards, rows, half), jnp.bfloat16),
            pltpu.VMEM((shards, rows, half), jnp.bfloat16),
            pltpu.VMEM((shards - 1, 2, rows, piece), jnp.bfloat16),
            pltpu.VMEM((shards, rows, half), jnp.bfloat16),
            pltpu.VMEM((rows, half), jnp.bfloat16),
            pltpu.VMEM((2, rows, piece), jnp.bfloat16),
            pltpu.VMEM((rows, columns), jnp.bfloat16),
            *[pltpu.VMEM((rows, columns), jnp.float32)] * 3,
            *[pltpu.VMEM(shape, jnp.bfloat16) for shape in halves * 2],
            sem((shards,)),
            sem((3,)),
            sem((shards - 1,)),
            sem((2, 4)),
            *[sem((shards,))] * 2,
            *[sem((shards, stages, 2))] * 2,
            *[sem((shards - 1,))] * 2,
            *[sem((shards - 1, 2))] * 2,
            *[sem((shards, stages, 2))] * 2,
            *[sem((shards,))] * 2,
        ],
        compiler_params=pltpu.CompilerParams(
            collective_id=0, has_side_effects=True, vmem_limit_bytes=28 * 1024 * 1024
        ),
        name="reduce_update_gather",
    )(*(pltpu.with_memory_space_constraint(x, pltpu.HBM) for x in (grads, master, moment_one, moment_two)))
    return pl.pallas_call(
        write_out,
        out_shape=outs,
        in_specs=[pl.BlockSpec(memory_space=pltpu.VMEM)] * 4,
        out_specs=[hbm] * 4,
        scratch_shapes=[sem((4,))],
        compiler_params=pltpu.CompilerParams(vmem_limit_bytes=16 * 1024 * 1024),
        name="write_out",
    )(*results)


def solution(mesh):
    placed = (
        P("replica", "shard", None, None),
        P("shard", None),
        P("shard", None),
        P("shard", None),
    )
    return jax.shard_map(
        functools.partial(local, mesh.shape["replica"], mesh.shape["shard"]),
        mesh=mesh,
        in_specs=placed,
        out_specs=(P("shard", None), P("shard", None), P("shard", None), P()),
        check_vma=False,
    )
```

```python
import functools

import jax
import jax.numpy as jnp
from jax import lax
from jax.experimental import pallas as pl
from jax.experimental.pallas import tpu as pltpu
from jax.sharding import PartitionSpec as P

STEP = 20
MESH = pl.DeviceIdType.MESH


def adam_update(total, master, moment_one, moment_two):
    first = 0.9 * moment_one + 0.1 * total
    second = 0.95 * moment_two + 0.05 * total * total
    first_hat = first / (1.0 - 0.9**STEP)
    second_hat = second / (1.0 - 0.95**STEP)
    updated = master - 0.0003 * (first_hat / (jnp.sqrt(second_hat) + 1e-08) + 0.1 * master)
    return (updated, first, second)


def aligned(offset, width):
    return pl.ds(pl.multiple_of(offset, width), width)


def over_tiles(rows, columns, body, widest=2048):
    width = min(columns, widest)
    across = columns // width

    def step(index, carry):
        body(pl.multiple_of(index // across * 16, 16), pl.multiple_of(index % across * width, width), width)
        return carry

    lax.fori_loop(0, rows // 16 * across, step, 0)


def kernel(
    replicas, shards, parts, grads, master, moment_one, moment_two,
    master_out, one_out, two_out, weights_out, *scratch,
):
    stages = replicas.bit_length() - 2
    (
        own, theirs, from_shard, held, total_pair, own_weights, row_weights, all_master, all_one, all_two,
    ) = scratch[:10]
    arrived = scratch[10 : 10 + stages]
    summed = scratch[10 + stages : 10 + 2 * stages]
    (
        load_sem, state_sem, store_sem, out_sem, core_send, core_recv, halve_send, halve_recv, shard_send, shard_recv,
        spread_send, spread_recv, join_send, join_recv, pair_send, pair_recv,
    ) = scratch[10 + 2 * stages :]

    rows = master.shape[0] // parts
    columns = master.shape[1]
    half = columns // 2
    stream = half // 2
    chunks = parts * shards
    me = lax.axis_index("replica")
    at = lax.axis_index("shard")
    bit = [me // (1 << b) % 2 for b in range(stages + 1)]
    partner = [me + (1 - 2 * bit[b]) * (1 << b) for b in range(stages + 1)]
    forward = list(range(1, stages + 1))
    orders = (forward, forward[::-1])

    def width(stage):
        return stream >> (stage + 1)

    def base(q, stage):
        offset = q * stream
        for u in range(stage + 1):
            offset = offset + bit[orders[q][u]] * width(u)
        return offset

    def remote(src, dst, send_sem, recv_sem, replica, shard):
        copy = pltpu.make_async_remote_copy(
            src_ref=src, dst_ref=dst, send_sem=send_sem, recv_sem=recv_sem,
            device_id=(replica, shard), device_id_type=MESH,
        )
        copy.start()
        return copy

    def tile(row, offset=0):
        return pl.ds(pl.multiple_of(row + offset, 16), 16)

    def span(offset, column, wide):
        return pl.ds(pl.multiple_of(offset + column, wide), wide)

    sent = []
    local = []

    def chunk_rows(part, shard):
        return aligned((shard * parts + part) * rows, rows)

    def reduced_rows(n):
        return chunk_rows(n // shards, lax.rem(at + 1 + n % shards, shards))

    loads = []
    for n in range(chunks):
        copy = pltpu.make_async_copy(
            grads.at[0, 0, reduced_rows(n), aligned(bit[0] * half, half)], own.at[n], load_sem.at[n]
        )
        copy.start()
        loads.append(copy)

    barrier = pltpu.get_barrier_semaphore()
    for other in partner:
        pl.semaphore_signal(barrier, inc=1, device_id=(other, at), device_id_type=MESH)
    for d in range(1, shards):
        pl.semaphore_signal(barrier, inc=1, device_id=(me, lax.rem(at + d, shards)), device_id_type=MESH)
    pl.semaphore_wait(barrier, len(partner) + shards - 1)

    core = []

    def start_core(n):
        core.append(
            remote(
                grads.at[0, 0, reduced_rows(n), aligned((1 - bit[0]) * half, half)],
                theirs.at[n], core_send.at[n], core_recv.at[n], partner[0], at,
            )
        )
        sent.append(core[n])

    for n in range(2):
        start_core(n)
    states = []
    for s, (source, target) in enumerate(((master, all_master), (moment_one, all_one), (moment_two, all_two))):
        copy = pltpu.make_async_copy(source, target, state_sem.at[s])
        copy.start()
        states.append(copy)
    halving = {}
    shard_copies = {part: [] for part in range(parts)}

    def start_halving(n, stage, q):
        wide = width(stage)
        b = orders[q][stage]
        if stage == 0:
            source = own.at[n, :, aligned(q * stream + (1 - bit[b]) * wide, wide)]
        else:
            source = summed[stage - 1].at[n, q, :, aligned((1 - bit[b]) * wide, wide)]
        halving[n, stage, q] = remote(
            source, arrived[stage].at[n, q], halve_send.at[n, stage, q], halve_recv.at[n, stage, q], partner[b], at
        )
        sent.append(halving[n, stage, q])

    def reduce(n, step):
        if step == 0:
            loads[n].wait()
            core[n].wait_recv()
            if n + 2 < chunks:
                start_core(n + 2)
            for q in range(2):

                def add(r, c, wide):
                    where = span(q * stream, c, wide)
                    own[n, tile(r), where] = own[n, tile(r), where] + theirs[n, tile(r), where]

                over_tiles(rows, stream, add)
                start_halving(n, 0, q)
            return
        stage = step - 1
        for q in range(2):
            halving[n, stage, q].wait_recv()
            kept = bit[orders[q][stage]] * width(stage)

            def add(r, c, wide):
                if stage == 0:
                    mine = own[n, tile(r), span(q * stream + kept, c, wide)]
                else:
                    mine = summed[stage - 1][n, q, tile(r), span(kept, c, wide)]
                summed[stage][n, q, tile(r), pl.ds(c, wide)] = mine + arrived[stage][n, q, tile(r), pl.ds(c, wide)]

            over_tiles(rows, width(stage), add)
            if step < stages:
                start_halving(n, step, q)
        part, i = divmod(n, shards)
        if step == stages and i < shards - 1:
            copy = remote(
                summed[stages - 1].at[n], from_shard.at[part, i], shard_send.at[part, i], shard_recv.at[part, i],
                me, lax.rem(at + 1 + i, shards),
            )
            shard_copies[part].append(copy)
            sent.append(copy)

    piece = width(stages - 1)
    joining = {}
    spread = {}
    pairs = {}
    todo = []

    def join(m, stage, q):
        where = aligned(base(q, stage), width(stage))
        joining[m, stage, q] = remote(
            held.at[m, :, where], held.at[m, :, where], join_send.at[m, stage, q], join_recv.at[m, stage, q],
            partner[orders[q][stage]], at,
        )
        sent.append(joining[m, stage, q])

    def own_piece(part):
        for copy in shard_copies[part]:
            copy.wait_recv()
        m = part * shards
        for q in range(2):
            offset = base(q, stages - 1)

            def finish(r, c, wide):
                total = summed[stages - 1][m + shards - 1, q, tile(r), pl.ds(c, wide)].astype(jnp.float32)
                for i in range(shards - 1):
                    total = total + from_shard[part, i, q, tile(r), pl.ds(c, wide)].astype(jnp.float32)
                held[m, tile(r), span(offset, c, wide)] = total.astype(jnp.bfloat16)

            over_tiles(rows, piece, finish, 512)
            join(m, stages - 1, q)
        if part == 0:
            for copy in states:
                copy.wait()
        for q in range(2):
            offset = base(q, stages - 1)

            def own_update(r, c, wide):
                total = held[m, tile(r), span(offset, c, wide)].astype(jnp.float32)
                row = tile(r, part * rows)
                where = span(bit[0] * half + offset, c, wide)
                updated, _, _ = adam_update(total, all_master[row, where], all_one[row, where], all_two[row, where])
                own_weights[part, q, tile(r), pl.ds(c, wide)] = updated.astype(jnp.bfloat16)

            over_tiles(rows, piece, own_update, 512)
        for d in range(1, shards):
            for q in range(2):
                spread[part, d, q] = remote(
                    own_weights.at[part, q], held.at[m + d, :, aligned(base(q, stages - 1), piece)],
                    spread_send.at[part, d - 1, q], spread_recv.at[part, d - 1, q], me, lax.rem(at + d, shards),
                )
                sent.append(spread[part, d, q])

    def update_rows(part, side, group):
        start = (bit[0] if side == 0 else 1 - bit[0]) * half
        m = part * shards
        if side == 1 and group == 0:
            pairs[m].wait_recv()

        def update(r, c, wide):
            r = pl.ds(group * 16, 16)
            total = held[m, r, pl.ds(c, wide)] if side == 0 else total_pair[part, r, pl.ds(c, wide)]
            row = pl.ds(part * rows + group * 16, 16)
            where = span(start, c, wide)
            updated, first, second = adam_update(
                total.astype(jnp.float32), all_master[row, where], all_one[row, where], all_two[row, where]
            )
            all_master[row, where] = updated
            all_one[row, where] = first
            all_two[row, where] = second
            row_weights[row, where] = updated.astype(jnp.bfloat16)

        over_tiles(16, half, update, 512)
        if group == rows // 16 - 1:
            block = pl.ds(part * rows, rows)
            where = aligned(start, half)
            targets = (
                (all_master, master_out.at[block, where]),
                (all_one, one_out.at[block, where]),
                (all_two, two_out.at[block, where]),
                (row_weights, weights_out.at[chunk_rows(part, at), where]),
            )
            for s, (source, target) in enumerate(targets):
                copy = pltpu.make_async_copy(source.at[block, where], target, out_sem.at[part, side, s])
                copy.start()
                local.append(copy)

    def gather(m, step):
        part, j = divmod(m, shards)
        for q in range(2):
            if step > 0:
                joining[m, stages - step, q].wait_recv()
            elif j > 0:
                spread[part, j, q].wait_recv()
            if step < stages and (j, step) != (0, 0):
                join(m, stages - 1 - step, q)
        if step < stages:
            return
        if j == 0:
            target = total_pair.at[part]
            todo.extend((part, side, group) for side in range(2) for group in range(rows // 16))
        else:
            target = weights_out.at[
                chunk_rows(part, lax.rem(at + shards - j, shards)), aligned(bit[0] * half, half)
            ]
            copy = pltpu.make_async_copy(held.at[m], target, store_sem.at[m])
            copy.start()
            local.append(copy)
        pairs[m] = remote(held.at[m], target, pair_send.at[m], pair_recv.at[m], partner[0], at)
        sent.append(pairs[m])

    ahead = 2

    def gather_tick(tick):
        for step in reversed(range(stages + 1)):
            if 0 <= tick - step * ahead < chunks:
                gather(tick - step * ahead, step)
                if todo:
                    update_rows(*todo.pop(0))

    ready = 0
    gathered = 0
    for tick in range(chunks + stages):
        for step in range(stages + 1):
            if 0 <= tick - step < chunks:
                reduce(tick - step, step)
        if tick == (ready + 1) * shards - 1 + stages:
            own_piece(ready)
            ready += 1
        if gathered < ready * shards:
            gather_tick(gathered)
            gathered += 1
    while gathered < chunks + stages * ahead:
        gather_tick(gathered)
        gathered += 1
    while todo:
        update_rows(*todo.pop(0))

    for m, pair in pairs.items():
        if m % shards:
            pair.wait_recv()
    for copy in local:
        copy.wait()
    for copy in sent:
        copy.wait_send()


def write_out(*refs):
    count = len(refs) // 2
    copies = [pltpu.make_async_copy(refs[k], refs[count + k], refs[-1].at[k]) for k in range(count)]
    for copy in copies:
        copy.start()
    for copy in copies:
        copy.wait()


def local(replicas, shards, grads, master, moment_one, moment_two):
    rows, columns = master.shape
    half = columns // 2
    stages = replicas.bit_length() - 2
    piece = half // 2 >> stages
    parts = 2 if rows % 32 == 0 else 1
    chunks = parts * shards
    part = rows // parts
    halves = [(chunks, 2, part, half // 2 >> (t + 1)) for t in range(stages)]
    sem = pltpu.SemaphoreType.DMA
    hbm = pl.BlockSpec(memory_space=pltpu.HBM)
    outs = tuple(
        jax.ShapeDtypeStruct(shape, dtype)
        for shape, dtype in [((rows, columns), jnp.float32)] * 3 + [((rows * shards, columns), jnp.bfloat16)]
    )
    results = pl.pallas_call(
        functools.partial(kernel, replicas, shards, parts),
        out_shape=outs,
        in_specs=[hbm] * 4,
        out_specs=[pl.BlockSpec(memory_space=pl.ANY)] * 4,
        scratch_shapes=[
            pltpu.VMEM((chunks, part, half), jnp.bfloat16),
            pltpu.VMEM((chunks, part, half), jnp.bfloat16),
            pltpu.VMEM((parts, shards - 1, 2, part, piece), jnp.bfloat16),
            pltpu.VMEM((chunks, part, half), jnp.bfloat16),
            pltpu.VMEM((parts, part, half), jnp.bfloat16),
            pltpu.VMEM((parts, 2, part, piece), jnp.bfloat16),
            pltpu.VMEM((rows, columns), jnp.bfloat16),
            *[pltpu.VMEM((rows, columns), jnp.float32)] * 3,
            *[pltpu.VMEM(shape, jnp.bfloat16) for shape in halves * 2],
            sem((chunks,)),
            sem((3,)),
            sem((chunks,)),
            sem((parts, 2, 4)),
            *[sem((chunks,))] * 2,
            *[sem((chunks, stages, 2))] * 2,
            *[sem((parts, shards - 1))] * 2,
            *[sem((parts, shards - 1, 2))] * 2,
            *[sem((chunks, stages, 2))] * 2,
            *[sem((chunks,))] * 2,
        ],
        compiler_params=pltpu.CompilerParams(
            collective_id=0, has_side_effects=True, vmem_limit_bytes=28 * 1024 * 1024
        ),
        name="reduce_update_gather",
    )(*(pltpu.with_memory_space_constraint(x, pltpu.HBM) for x in (grads, master, moment_one, moment_two)))
    return pl.pallas_call(
        write_out,
        out_shape=outs,
        in_specs=[pl.BlockSpec(memory_space=pltpu.VMEM)] * 4,
        out_specs=[hbm] * 4,
        scratch_shapes=[sem((4,))],
        compiler_params=pltpu.CompilerParams(vmem_limit_bytes=16 * 1024 * 1024),
        name="write_out",
    )(*results)


def solution(mesh):
    placed = (
        P("replica", "shard", None, None),
        P("shard", None),
        P("shard", None),
        P("shard", None),
    )
    return jax.shard_map(
        functools.partial(local, mesh.shape["replica"], mesh.shape["shard"]),
        mesh=mesh,
        in_specs=placed,
        out_specs=(P("shard", None), P("shard", None), P("shard", None), P()),
        check_vma=False,
    )
```

```python
import functools

import jax
import jax.numpy as jnp
from jax import lax
from jax.experimental import pallas as pl
from jax.experimental.pallas import tpu as pltpu
from jax.sharding import PartitionSpec as P

STEP = 20
MESH = pl.DeviceIdType.MESH


def adam_update(total, master, moment_one, moment_two):
    first = 0.9 * moment_one + 0.1 * total
    second = 0.95 * moment_two + 0.05 * total * total
    first_hat = first / (1.0 - 0.9**STEP)
    second_hat = second / (1.0 - 0.95**STEP)
    updated = master - 0.0003 * (first_hat / (jnp.sqrt(second_hat) + 1e-08) + 0.1 * master)
    return (updated, first, second)


def aligned(offset, width):
    return pl.ds(pl.multiple_of(offset, width), width)


def over_tiles(rows, columns, body, widest=2048):
    width = min(columns, widest)
    across = columns // width

    def step(index, carry):
        body(pl.multiple_of(index // across * 16, 16), pl.multiple_of(index % across * width, width), width)
        return carry

    lax.fori_loop(0, rows // 16 * across, step, 0)


CORE_AHEAD = 2


def plan(shards, stages, parts, groups, kib, hop=1.5, rate=100.0, issue=0.1):
    chunks = parts * shards
    now, free, arrives = 2.0, {}, {}
    left = [shards] * parts

    def send(key, link, amount, speed):
        nonlocal now
        now += issue
        free[link] = max(now, free.get(link, 0.0)) + amount * 1.024 / speed
        arrives[key] = free[link] + hop

    def core(n):
        if n < chunks:
            send(("core", n), "core", kib, 6 * rate)

    def needs(kind, n, step):
        if kind == "reduce":
            return [("core", n)] if step == 0 else [("halve", n, step - 1, q) for q in range(2)]
        if kind == "own":
            return [("shard", n, i) for i in range(shards - 1)]
        if kind == "gather":
            return [("spread", n)] if step == 0 else [("join", n, step - 1, q) for q in range(2)]
        return [("pair", n * shards)] if step else []

    def take(kind, n, step):
        nonlocal now
        if kind == "reduce":
            if step == 0:
                core(n + CORE_AHEAD)
            for q in range(2):
                now += 0.4 / parts / 2**step
                if step < stages:
                    send(("halve", n, step, q), (q + step) % stages, kib / 2 ** (step + 1), rate)
            if step < stages:
                return [("reduce", n, step + 1)]
            part, i = divmod(n, shards)
            left[part] -= 1
            if i < shards - 1:
                send(("shard", part, i), "shard", min(i + 1, shards - 1 - i) * kib / 2**stages, rate)
            return [] if left[part] else [("own", part, 0)]
        if kind == "own":
            for q in range(2):
                now += 0.2 / parts
                send(("join", n * shards, 0, q), (q + stages - 1) % stages, kib / 2**stages, rate)
            now += 0.8 / parts
            for d in range(1, shards):
                send(("spread", n * shards + d), "shard", min(d, shards - d) * kib / 2**stages, rate)
            return [("gather", n * shards, 1)] + [("gather", n * shards + d, 0) for d in range(1, shards)]
        if kind == "gather":
            if step < stages:
                for q in range(2):
                    send(("join", n, step, q), (q + stages - 1 - step) % stages, kib / 2 ** (stages - step), rate)
                return [("gather", n, step + 1)]
            send(("pair", n), "core", kib, 6 * rate)
            if n % shards:
                return []
            return [("update", n // shards, side, group) for side in range(2) for group in range(groups)]
        now += 0.5
        return []

    for n in range(CORE_AHEAD):
        core(n)
    ready = [("reduce", n, 0) for n in range(chunks)]
    order = []
    while ready:
        best = None
        for op in ready:
            waits = needs(*op[:3])
            if any(key not in arrives for key in waits):
                continue
            start = max([now] + [arrives[key] for key in waits])
            if op[0] == "update":
                place = (start + 0.5, 2, op[1:])
            else:
                place = (start, 1 if op[0] == "gather" else 0, (op[1], -op[2]))
            if best is None or place < best[0]:
                best = (place, start, op)
        now = best[1]
        ready.remove(best[2])
        order.append(best[2])
        ready += take(*best[2][:3])
    return order


def kernel(
    replicas, shards, parts, grads, master, moment_one, moment_two,
    master_out, one_out, two_out, weights_out, *scratch,
):
    stages = replicas.bit_length() - 2
    (
        own, theirs, from_shard, held, total_pair, own_weights, row_weights, all_master, all_one, all_two,
    ) = scratch[:10]
    arrived = scratch[10 : 10 + stages]
    summed = scratch[10 + stages : 10 + 2 * stages]
    (
        load_sem, state_sem, store_sem, out_sem, core_send, core_recv, halve_send, halve_recv, shard_send, shard_recv,
        spread_send, spread_recv, join_send, join_recv, pair_send, pair_recv,
    ) = scratch[10 + 2 * stages :]

    rows = master.shape[0] // parts
    columns = master.shape[1]
    half = columns // 2
    stream = half // 2
    chunks = parts * shards
    me = lax.axis_index("replica")
    at = lax.axis_index("shard")
    bit = [me // (1 << b) % 2 for b in range(stages + 1)]
    partner = [me + (1 - 2 * bit[b]) * (1 << b) for b in range(stages + 1)]
    forward = list(range(1, stages + 1))
    orders = (forward, forward[::-1])

    def width(stage):
        return stream >> (stage + 1)

    def base(q, stage):
        offset = q * stream
        for u in range(stage + 1):
            offset = offset + bit[orders[q][u]] * width(u)
        return offset

    def remote(src, dst, send_sem, recv_sem, replica, shard):
        copy = pltpu.make_async_remote_copy(
            src_ref=src, dst_ref=dst, send_sem=send_sem, recv_sem=recv_sem,
            device_id=(replica, shard), device_id_type=MESH,
        )
        copy.start()
        return copy

    def tile(row, offset=0):
        return pl.ds(pl.multiple_of(row + offset, 16), 16)

    def span(offset, column, wide):
        return pl.ds(pl.multiple_of(offset + column, wide), wide)

    sent = []
    local = []

    def chunk_rows(part, shard):
        return aligned((shard * parts + part) * rows, rows)

    def reduced_rows(n):
        return chunk_rows(n // shards, lax.rem(at + 1 + n % shards, shards))

    loads = []
    for n in range(chunks):
        copy = pltpu.make_async_copy(
            grads.at[0, 0, reduced_rows(n), aligned(bit[0] * half, half)], own.at[n], load_sem.at[n]
        )
        copy.start()
        loads.append(copy)

    barrier = pltpu.get_barrier_semaphore()
    for other in partner:
        pl.semaphore_signal(barrier, inc=1, device_id=(other, at), device_id_type=MESH)
    for d in range(1, shards):
        pl.semaphore_signal(barrier, inc=1, device_id=(me, lax.rem(at + d, shards)), device_id_type=MESH)
    pl.semaphore_wait(barrier, len(partner) + shards - 1)

    core = {}

    def start_core(n):
        core[n] = remote(
            grads.at[0, 0, reduced_rows(n), aligned((1 - bit[0]) * half, half)],
            theirs.at[n], core_send.at[n], core_recv.at[n], partner[0], at,
        )
        sent.append(core[n])

    for n in range(CORE_AHEAD):
        start_core(n)
    states = []
    for s, (source, target) in enumerate(((master, all_master), (moment_one, all_one), (moment_two, all_two))):
        copy = pltpu.make_async_copy(source, target, state_sem.at[s])
        copy.start()
        states.append(copy)
    halving = {}
    shard_copies = {part: [] for part in range(parts)}

    def start_halving(n, stage, q):
        wide = width(stage)
        b = orders[q][stage]
        if stage == 0:
            source = own.at[n, :, aligned(q * stream + (1 - bit[b]) * wide, wide)]
        else:
            source = summed[stage - 1].at[n, q, :, aligned((1 - bit[b]) * wide, wide)]
        halving[n, stage, q] = remote(
            source, arrived[stage].at[n, q], halve_send.at[n, stage, q], halve_recv.at[n, stage, q], partner[b], at
        )
        sent.append(halving[n, stage, q])

    def reduce(n, step):
        if step == 0:
            loads[n].wait()
            core[n].wait_recv()
            if n + CORE_AHEAD < chunks:
                start_core(n + CORE_AHEAD)
            for q in range(2):

                def add(r, c, wide):
                    where = span(q * stream, c, wide)
                    own[n, tile(r), where] = own[n, tile(r), where] + theirs[n, tile(r), where]

                over_tiles(rows, stream, add)
                start_halving(n, 0, q)
            return
        stage = step - 1
        for q in range(2):
            halving[n, stage, q].wait_recv()
            kept = bit[orders[q][stage]] * width(stage)

            def add(r, c, wide):
                if stage == 0:
                    mine = own[n, tile(r), span(q * stream + kept, c, wide)]
                else:
                    mine = summed[stage - 1][n, q, tile(r), span(kept, c, wide)]
                summed[stage][n, q, tile(r), pl.ds(c, wide)] = mine + arrived[stage][n, q, tile(r), pl.ds(c, wide)]

            over_tiles(rows, width(stage), add)
            if step < stages:
                start_halving(n, step, q)
        part, i = divmod(n, shards)
        if step == stages and i < shards - 1:
            copy = remote(
                summed[stages - 1].at[n], from_shard.at[part, i], shard_send.at[part, i], shard_recv.at[part, i],
                me, lax.rem(at + 1 + i, shards),
            )
            shard_copies[part].append(copy)
            sent.append(copy)

    piece = width(stages - 1)
    joining = {}
    spread = {}
    pairs = {}

    def join(m, stage, q):
        where = aligned(base(q, stage), width(stage))
        joining[m, stage, q] = remote(
            held.at[m, :, where], held.at[m, :, where], join_send.at[m, stage, q], join_recv.at[m, stage, q],
            partner[orders[q][stage]], at,
        )
        sent.append(joining[m, stage, q])

    def own_piece(part, step):
        for copy in shard_copies[part]:
            copy.wait_recv()
        m = part * shards
        for q in range(2):
            offset = base(q, stages - 1)

            def finish(r, c, wide):
                total = summed[stages - 1][m + shards - 1, q, tile(r), pl.ds(c, wide)].astype(jnp.float32)
                for i in range(shards - 1):
                    total = total + from_shard[part, i, q, tile(r), pl.ds(c, wide)].astype(jnp.float32)
                held[m, tile(r), span(offset, c, wide)] = total.astype(jnp.bfloat16)

            over_tiles(rows, piece, finish, 512)
            join(m, stages - 1, q)
        while states:
            states.pop().wait()
        for q in range(2):
            offset = base(q, stages - 1)

            def own_update(r, c, wide):
                total = held[m, tile(r), span(offset, c, wide)].astype(jnp.float32)
                row = tile(r, part * rows)
                where = span(bit[0] * half + offset, c, wide)
                updated, _, _ = adam_update(total, all_master[row, where], all_one[row, where], all_two[row, where])
                own_weights[part, q, tile(r), pl.ds(c, wide)] = updated.astype(jnp.bfloat16)

            over_tiles(rows, piece, own_update, 512)
        for d in range(1, shards):
            for q in range(2):
                spread[part, d, q] = remote(
                    own_weights.at[part, q], held.at[m + d, :, aligned(base(q, stages - 1), piece)],
                    spread_send.at[part, d - 1, q], spread_recv.at[part, d - 1, q], me, lax.rem(at + d, shards),
                )
                sent.append(spread[part, d, q])

    def update_rows(part, side, group):
        start = (bit[0] if side == 0 else 1 - bit[0]) * half
        m = part * shards
        if side == 1 and group == 0:
            pairs[m].wait_recv()

        def update(r, c, wide):
            r = pl.ds(group * 16, 16)
            total = held[m, r, pl.ds(c, wide)] if side == 0 else total_pair[part, r, pl.ds(c, wide)]
            row = pl.ds(part * rows + group * 16, 16)
            where = span(start, c, wide)
            updated, first, second = adam_update(
                total.astype(jnp.float32), all_master[row, where], all_one[row, where], all_two[row, where]
            )
            all_master[row, where] = updated
            all_one[row, where] = first
            all_two[row, where] = second
            row_weights[row, where] = updated.astype(jnp.bfloat16)

        over_tiles(16, half, update, 512)
        if group == rows // 16 - 1:
            block = pl.ds(part * rows, rows)
            where = aligned(start, half)
            targets = (
                (all_master, master_out.at[block, where]),
                (all_one, one_out.at[block, where]),
                (all_two, two_out.at[block, where]),
                (row_weights, weights_out.at[chunk_rows(part, at), where]),
            )
            for s, (source, target) in enumerate(targets):
                copy = pltpu.make_async_copy(source.at[block, where], target, out_sem.at[part, side, s])
                copy.start()
                local.append(copy)

    def gather(m, step):
        part, j = divmod(m, shards)
        for q in range(2):
            if step > 0:
                joining[m, stages - step, q].wait_recv()
            else:
                spread[part, j, q].wait_recv()
            if step < stages:
                join(m, stages - 1 - step, q)
        if step < stages:
            return
        if j == 0:
            target = total_pair.at[part]
        else:
            target = weights_out.at[
                chunk_rows(part, lax.rem(at + shards - j, shards)), aligned(bit[0] * half, half)
            ]
            copy = pltpu.make_async_copy(held.at[m], target, store_sem.at[m])
            copy.start()
            local.append(copy)
        pairs[m] = remote(held.at[m], target, pair_send.at[m], pair_recv.at[m], partner[0], at)
        sent.append(pairs[m])

    steps = {"reduce": reduce, "own": own_piece, "gather": gather, "update": update_rows}
    kib = rows * half * 2 // 1024
    for kind, *which in plan(shards, stages, parts, rows // 16, kib):
        steps[kind](*which)

    for m, pair in pairs.items():
        if m % shards:
            pair.wait_recv()
    for copy in local:
        copy.wait()
    for copy in sent:
        copy.wait_send()


def write_out(*refs):
    count = len(refs) // 2
    copies = [pltpu.make_async_copy(refs[k], refs[count + k], refs[-1].at[k]) for k in range(count)]
    for copy in copies:
        copy.start()
    for copy in copies:
        copy.wait()


def local(replicas, shards, grads, master, moment_one, moment_two):
    rows, columns = master.shape
    half = columns // 2
    stages = replicas.bit_length() - 2
    piece = half // 2 >> stages
    parts = 2 if rows % 32 == 0 else 1
    chunks = parts * shards
    part = rows // parts
    halves = [(chunks, 2, part, half // 2 >> (t + 1)) for t in range(stages)]
    sem = pltpu.SemaphoreType.DMA
    hbm = pl.BlockSpec(memory_space=pltpu.HBM)
    outs = tuple(
        jax.ShapeDtypeStruct(shape, dtype)
        for shape, dtype in [((rows, columns), jnp.float32)] * 3 + [((rows * shards, columns), jnp.bfloat16)]
    )
    results = pl.pallas_call(
        functools.partial(kernel, replicas, shards, parts),
        out_shape=outs,
        in_specs=[hbm] * 4,
        out_specs=[pl.BlockSpec(memory_space=pl.ANY)] * 4,
        scratch_shapes=[
            pltpu.VMEM((chunks, part, half), jnp.bfloat16),
            pltpu.VMEM((chunks, part, half), jnp.bfloat16),
            pltpu.VMEM((parts, shards - 1, 2, part, piece), jnp.bfloat16),
            pltpu.VMEM((chunks, part, half), jnp.bfloat16),
            pltpu.VMEM((parts, part, half), jnp.bfloat16),
            pltpu.VMEM((parts, 2, part, piece), jnp.bfloat16),
            pltpu.VMEM((rows, columns), jnp.bfloat16),
            *[pltpu.VMEM((rows, columns), jnp.float32)] * 3,
            *[pltpu.VMEM(shape, jnp.bfloat16) for shape in halves * 2],
            sem((chunks,)),
            sem((3,)),
            sem((chunks,)),
            sem((parts, 2, 4)),
            *[sem((chunks,))] * 2,
            *[sem((chunks, stages, 2))] * 2,
            *[sem((parts, shards - 1))] * 2,
            *[sem((parts, shards - 1, 2))] * 2,
            *[sem((chunks, stages, 2))] * 2,
            *[sem((chunks,))] * 2,
        ],
        compiler_params=pltpu.CompilerParams(
            collective_id=0, has_side_effects=True, vmem_limit_bytes=28 * 1024 * 1024
        ),
        name="reduce_update_gather",
    )(*(pltpu.with_memory_space_constraint(x, pltpu.HBM) for x in (grads, master, moment_one, moment_two)))
    return pl.pallas_call(
        write_out,
        out_shape=outs,
        in_specs=[pl.BlockSpec(memory_space=pltpu.VMEM)] * 4,
        out_specs=[hbm] * 4,
        scratch_shapes=[sem((4,))],
        compiler_params=pltpu.CompilerParams(vmem_limit_bytes=16 * 1024 * 1024),
        name="write_out",
    )(*results)


def solution(mesh):
    placed = (
        P("replica", "shard", None, None),
        P("shard", None),
        P("shard", None),
        P("shard", None),
    )
    return jax.shard_map(
        functools.partial(local, mesh.shape["replica"], mesh.shape["shard"]),
        mesh=mesh,
        in_specs=placed,
        out_specs=(P("shard", None), P("shard", None), P("shard", None), P()),
        check_vma=False,
    )
```

```python
import functools

import jax
import jax.numpy as jnp
from jax import lax
from jax.experimental import pallas as pl
from jax.experimental.pallas import tpu as pltpu
from jax.sharding import PartitionSpec as P

STEP = 20
MESH = pl.DeviceIdType.MESH


def adam_update(total, master, moment_one, moment_two):
    first = 0.9 * moment_one + 0.1 * total
    second = 0.95 * moment_two + 0.05 * (total * total)
    second_hat = second * (1.0 / (1.0 - 0.95**STEP))
    root = second_hat * lax.rsqrt(second_hat)
    step = (0.0003 / (1.0 - 0.9**STEP)) * first / (root + 1e-08)
    updated = (1.0 - 0.0003 * 0.1) * master - step
    return (updated, first, second)


def aligned(offset, width):
    return pl.ds(pl.multiple_of(offset, width), width)


def over_tiles(rows, columns, body, widest=2048):
    width = min(columns, widest)
    across = columns // width

    def step(index, carry):
        body(pl.multiple_of(index // across * 16, 16), pl.multiple_of(index % across * width, width), width)
        return carry

    lax.fori_loop(0, rows // 16 * across, step, 0)


def kernel(
    replicas, shards, parts, grads, master, moment_one, moment_two,
    master_out, one_out, two_out, weights_out, *scratch,
):
    stages = replicas.bit_length() - 2
    (
        own, theirs, from_shard, held, total_pair, own_weights, row_weights, all_master, all_one, all_two,
    ) = scratch[:10]
    arrived = scratch[10 : 10 + stages]
    summed = scratch[10 + stages : 10 + 2 * stages]
    (
        load_sem, state_sem, store_sem, out_sem, core_send, core_recv, halve_send, halve_recv, shard_send, shard_recv,
        spread_send, spread_recv, join_send, join_recv, pair_send, pair_recv,
    ) = scratch[10 + 2 * stages :]

    rows = master.shape[0] // parts
    columns = master.shape[1]
    half = columns // 2
    stream = half // 2
    chunks = parts * shards
    me = lax.axis_index("replica")
    at = lax.axis_index("shard")
    bit = [me // (1 << b) % 2 for b in range(stages + 1)]
    partner = [me + (1 - 2 * bit[b]) * (1 << b) for b in range(stages + 1)]
    forward = list(range(1, stages + 1))
    orders = (forward, forward[::-1])

    def width(stage):
        return stream >> (stage + 1)

    def base(q, stage):
        offset = q * stream
        for u in range(stage + 1):
            offset = offset + bit[orders[q][u]] * width(u)
        return offset

    def remote(src, dst, send_sem, recv_sem, replica, shard):
        copy = pltpu.make_async_remote_copy(
            src_ref=src, dst_ref=dst, send_sem=send_sem, recv_sem=recv_sem,
            device_id=(replica, shard), device_id_type=MESH,
        )
        copy.start()
        return copy

    def tile(row, offset=0):
        return pl.ds(pl.multiple_of(row + offset, 16), 16)

    def span(offset, column, wide):
        return pl.ds(pl.multiple_of(offset + column, wide), wide)

    sent = []
    local = []

    def chunk_rows(part, shard):
        return aligned((shard * parts + part) * rows, rows)

    def reduced_rows(n):
        return chunk_rows(n // shards, lax.rem(at + 1 + n % shards, shards))

    loads = []
    for n in range(chunks):
        copy = pltpu.make_async_copy(
            grads.at[0, 0, reduced_rows(n), aligned(bit[0] * half, half)], own.at[n], load_sem.at[n]
        )
        copy.start()
        loads.append(copy)

    barrier = pltpu.get_barrier_semaphore()
    for other in partner:
        pl.semaphore_signal(barrier, inc=1, device_id=(other, at), device_id_type=MESH)
    for d in range(1, shards):
        pl.semaphore_signal(barrier, inc=1, device_id=(me, lax.rem(at + d, shards)), device_id_type=MESH)
    pl.semaphore_wait(barrier, len(partner) + shards - 1)

    core = []

    def start_core(n):
        core.append(
            remote(
                grads.at[0, 0, reduced_rows(n), aligned((1 - bit[0]) * half, half)],
                theirs.at[n], core_send.at[n], core_recv.at[n], partner[0], at,
            )
        )
        sent.append(core[n])

    for n in range(2):
        start_core(n)
    states = []
    for s, (source, target) in enumerate(((master, all_master), (moment_one, all_one), (moment_two, all_two))):
        copy = pltpu.make_async_copy(source, target, state_sem.at[s])
        copy.start()
        states.append(copy)
    halving = {}
    shard_copies = {part: [] for part in range(parts)}

    def start_halving(n, stage, q):
        wide = width(stage)
        b = orders[q][stage]
        if stage == 0:
            source = own.at[n, :, aligned(q * stream + (1 - bit[b]) * wide, wide)]
        else:
            source = summed[stage - 1].at[n, q, :, aligned((1 - bit[b]) * wide, wide)]
        halving[n, stage, q] = remote(
            source, arrived[stage].at[n, q], halve_send.at[n, stage, q], halve_recv.at[n, stage, q], partner[b], at
        )
        sent.append(halving[n, stage, q])

    def reduce(n, step):
        if step == 0:
            loads[n].wait()
            core[n].wait_recv()
            if n + 2 < chunks:
                start_core(n + 2)
            for q in range(2):

                def add(r, c, wide):
                    where = span(q * stream, c, wide)
                    own[n, tile(r), where] = own[n, tile(r), where] + theirs[n, tile(r), where]

                over_tiles(rows, stream, add)
                start_halving(n, 0, q)
            return
        stage = step - 1
        for q in range(2):
            halving[n, stage, q].wait_recv()
            kept = bit[orders[q][stage]] * width(stage)

            def add(r, c, wide):
                if stage == 0:
                    mine = own[n, tile(r), span(q * stream + kept, c, wide)]
                else:
                    mine = summed[stage - 1][n, q, tile(r), span(kept, c, wide)]
                summed[stage][n, q, tile(r), pl.ds(c, wide)] = mine + arrived[stage][n, q, tile(r), pl.ds(c, wide)]

            over_tiles(rows, width(stage), add)
            if step < stages:
                start_halving(n, step, q)
        part, i = divmod(n, shards)
        if step == stages and i < shards - 1:
            copy = remote(
                summed[stages - 1].at[n], from_shard.at[part, i], shard_send.at[part, i], shard_recv.at[part, i],
                me, lax.rem(at + 1 + i, shards),
            )
            shard_copies[part].append(copy)
            sent.append(copy)

    piece = width(stages - 1)
    joining = {}
    spread = {}
    pairs = {}
    todo = []

    def join(m, stage, q):
        where = aligned(base(q, stage), width(stage))
        joining[m, stage, q] = remote(
            held.at[m, :, where], held.at[m, :, where], join_send.at[m, stage, q], join_recv.at[m, stage, q],
            partner[orders[q][stage]], at,
        )
        sent.append(joining[m, stage, q])

    def own_piece(part):
        for copy in shard_copies[part]:
            copy.wait_recv()
        m = part * shards
        for q in range(2):
            offset = base(q, stages - 1)

            def finish(r, c, wide):
                total = summed[stages - 1][m + shards - 1, q, tile(r), pl.ds(c, wide)].astype(jnp.float32)
                for i in range(shards - 1):
                    total = total + from_shard[part, i, q, tile(r), pl.ds(c, wide)].astype(jnp.float32)
                held[m, tile(r), span(offset, c, wide)] = total.astype(jnp.bfloat16)

            over_tiles(rows, piece, finish)
            join(m, stages - 1, q)
        if part == 0:
            for copy in states:
                copy.wait()
        for q in range(2):
            offset = base(q, stages - 1)

            def own_update(r, c, wide):
                total = held[m, tile(r), span(offset, c, wide)].astype(jnp.float32)
                row = tile(r, part * rows)
                where = span(bit[0] * half + offset, c, wide)
                updated, _, _ = adam_update(total, all_master[row, where], all_one[row, where], all_two[row, where])
                own_weights[part, q, tile(r), pl.ds(c, wide)] = updated.astype(jnp.bfloat16)

            over_tiles(rows, piece, own_update)
        for d in range(1, shards):
            for q in range(2):
                spread[part, d, q] = remote(
                    own_weights.at[part, q], held.at[m + d, :, aligned(base(q, stages - 1), piece)],
                    spread_send.at[part, d - 1, q], spread_recv.at[part, d - 1, q], me, lax.rem(at + d, shards),
                )
                sent.append(spread[part, d, q])

    def update_rows(part, side, group, place):
        start = (bit[0] if side == 0 else 1 - bit[0]) * half
        m = part * shards
        if side == 1 and group == 0 and place == 0:
            pairs[m].wait_recv()

        def update(r, c, wide):
            r = pl.ds(group * 16, 16)
            here = span(place * stream, c, wide)
            total = held[m, r, here] if side == 0 else total_pair[part, r, here]
            row = pl.ds(part * rows + group * 16, 16)
            where = span(start + place * stream, c, wide)
            updated, first, second = adam_update(
                total.astype(jnp.float32), all_master[row, where], all_one[row, where], all_two[row, where]
            )
            all_master[row, where] = updated
            all_one[row, where] = first
            all_two[row, where] = second
            row_weights[row, where] = updated.astype(jnp.bfloat16)

        over_tiles(16, stream, update, 1024)
        if group == rows // 16 - 1 and place == 1:
            block = pl.ds(part * rows, rows)
            where = aligned(start, half)
            targets = (
                (all_master, master_out.at[block, where]),
                (all_one, one_out.at[block, where]),
                (all_two, two_out.at[block, where]),
                (row_weights, weights_out.at[chunk_rows(part, at), where]),
            )
            for s, (source, target) in enumerate(targets):
                copy = pltpu.make_async_copy(source.at[block, where], target, out_sem.at[part, side, s])
                copy.start()
                local.append(copy)

    def gather(m, step):
        part, j = divmod(m, shards)
        for q in range(2):
            if step > 0:
                joining[m, stages - step, q].wait_recv()
            elif j > 0:
                spread[part, j, q].wait_recv()
            if step < stages and (j, step) != (0, 0):
                join(m, stages - 1 - step, q)
        if step < stages:
            return
        if j == 0:
            target = total_pair.at[part]
            todo.extend(
                (part, side, group, place) for side in range(2) for group in range(rows // 16) for place in range(2)
            )
        else:
            target = weights_out.at[
                chunk_rows(part, lax.rem(at + shards - j, shards)), aligned(bit[0] * half, half)
            ]
            copy = pltpu.make_async_copy(held.at[m], target, store_sem.at[m])
            copy.start()
            local.append(copy)
        pairs[m] = remote(held.at[m], target, pair_send.at[m], pair_recv.at[m], partner[0], at)
        sent.append(pairs[m])

    ahead = 2

    def gather_tick(tick):
        for step in reversed(range(stages + 1)):
            if 0 <= tick - step * ahead < chunks:
                gather(tick - step * ahead, step)
                if todo:
                    update_rows(*todo.pop(0))

    ready = 0
    gathered = 0
    for tick in range(chunks + stages):
        for step in range(stages + 1):
            if 0 <= tick - step < chunks:
                reduce(tick - step, step)
        if tick == (ready + 1) * shards - 1 + stages:
            own_piece(ready)
            ready += 1
        if gathered < ready * shards:
            gather_tick(gathered)
            gathered += 1
    while gathered < chunks + stages * ahead:
        gather_tick(gathered)
        gathered += 1
    while todo:
        update_rows(*todo.pop(0))

    for m, pair in pairs.items():
        if m % shards:
            pair.wait_recv()
    for copy in local:
        copy.wait()
    for copy in sent:
        copy.wait_send()


def write_out(*refs):
    count = len(refs) // 2
    copies = [pltpu.make_async_copy(refs[k], refs[count + k], refs[-1].at[k]) for k in range(count)]
    for copy in copies:
        copy.start()
    for copy in copies:
        copy.wait()


def local(replicas, shards, grads, master, moment_one, moment_two):
    rows, columns = master.shape
    half = columns // 2
    stages = replicas.bit_length() - 2
    piece = half // 2 >> stages
    parts = 2 if rows % 32 == 0 else 1
    chunks = parts * shards
    part = rows // parts
    halves = [(chunks, 2, part, half // 2 >> (t + 1)) for t in range(stages)]
    sem = pltpu.SemaphoreType.DMA
    hbm = pl.BlockSpec(memory_space=pltpu.HBM)
    outs = tuple(
        jax.ShapeDtypeStruct(shape, dtype)
        for shape, dtype in [((rows, columns), jnp.float32)] * 3 + [((rows * shards, columns), jnp.bfloat16)]
    )
    results = pl.pallas_call(
        functools.partial(kernel, replicas, shards, parts),
        out_shape=outs,
        in_specs=[hbm] * 4,
        out_specs=[pl.BlockSpec(memory_space=pl.ANY)] * 4,
        scratch_shapes=[
            pltpu.VMEM((chunks, part, half), jnp.bfloat16),
            pltpu.VMEM((chunks, part, half), jnp.bfloat16),
            pltpu.VMEM((parts, shards - 1, 2, part, piece), jnp.bfloat16),
            pltpu.VMEM((chunks, part, half), jnp.bfloat16),
            pltpu.VMEM((parts, part, half), jnp.bfloat16),
            pltpu.VMEM((parts, 2, part, piece), jnp.bfloat16),
            pltpu.VMEM((rows, columns), jnp.bfloat16),
            *[pltpu.VMEM((rows, columns), jnp.float32)] * 3,
            *[pltpu.VMEM(shape, jnp.bfloat16) for shape in halves * 2],
            sem((chunks,)),
            sem((3,)),
            sem((chunks,)),
            sem((parts, 2, 4)),
            *[sem((chunks,))] * 2,
            *[sem((chunks, stages, 2))] * 2,
            *[sem((parts, shards - 1))] * 2,
            *[sem((parts, shards - 1, 2))] * 2,
            *[sem((chunks, stages, 2))] * 2,
            *[sem((chunks,))] * 2,
        ],
        compiler_params=pltpu.CompilerParams(
            collective_id=0, has_side_effects=True, vmem_limit_bytes=28 * 1024 * 1024
        ),
        name="reduce_update_gather",
    )(*(pltpu.with_memory_space_constraint(x, pltpu.HBM) for x in (grads, master, moment_one, moment_two)))
    return pl.pallas_call(
        write_out,
        out_shape=outs,
        in_specs=[pl.BlockSpec(memory_space=pltpu.VMEM)] * 4,
        out_specs=[hbm] * 4,
        scratch_shapes=[sem((4,))],
        compiler_params=pltpu.CompilerParams(vmem_limit_bytes=16 * 1024 * 1024),
        name="write_out",
    )(*results)


def solution(mesh):
    placed = (
        P("replica", "shard", None, None),
        P("shard", None),
        P("shard", None),
        P("shard", None),
    )
    return jax.shard_map(
        functools.partial(local, mesh.shape["replica"], mesh.shape["shard"]),
        mesh=mesh,
        in_specs=placed,
        out_specs=(P("shard", None), P("shard", None), P("shard", None), P()),
        check_vma=False,
    )
```

```python
import functools

import jax
import jax.numpy as jnp
from jax import lax
from jax.experimental import pallas as pl
from jax.experimental.pallas import tpu as pltpu
from jax.sharding import PartitionSpec as P

STEP = 20
MESH = pl.DeviceIdType.MESH


def adam_update(total, master, moment_one, moment_two):
    first = 0.9 * moment_one + 0.1 * total
    second = 0.95 * moment_two + 0.05 * (total * total)
    second_hat = second * (1.0 / (1.0 - 0.95**STEP))
    root = second_hat * lax.rsqrt(second_hat)
    step = (0.0003 / (1.0 - 0.9**STEP)) * first / (root + 1e-08)
    updated = (1.0 - 0.0003 * 0.1) * master - step
    return (updated, first, second)


def aligned(offset, width):
    return pl.ds(pl.multiple_of(offset, width), width)


def over_tiles(rows, columns, body, widest=2048):
    width = min(columns, widest)
    across = columns // width

    def step(index, carry):
        body(pl.multiple_of(index // across * 16, 16), pl.multiple_of(index % across * width, width), width)
        return carry

    lax.fori_loop(0, rows // 16 * across, step, 0)


def kernel(
    replicas, shards, parts, grads, master, moment_one, moment_two,
    master_out, one_out, two_out, weights_out, *scratch,
):
    stages = replicas.bit_length() - 2
    (
        own, theirs, from_shard, held, total_pair, own_weights, row_weights, all_master, all_one, all_two,
    ) = scratch[:10]
    arrived = scratch[10 : 10 + stages]
    summed = scratch[10 + stages : 10 + 2 * stages]
    (
        load_sem, state_sem, store_sem, out_sem, core_send, core_recv, halve_send, halve_recv, shard_send, shard_recv,
        spread_send, spread_recv, join_send, join_recv, pair_send, pair_recv,
    ) = scratch[10 + 2 * stages :]

    rows = master.shape[0] // parts
    columns = master.shape[1]
    half = columns // 2
    stream = half // 2
    chunks = parts * shards
    me = lax.axis_index("replica")
    at = lax.axis_index("shard")
    bit = [me // (1 << b) % 2 for b in range(stages + 1)]
    partner = [me + (1 - 2 * bit[b]) * (1 << b) for b in range(stages + 1)]
    forward = list(range(1, stages + 1))
    orders = (forward, forward[::-1])

    def width(stage):
        return stream >> (stage + 1)

    def base(q, stage):
        offset = q * stream
        for u in range(stage + 1):
            offset = offset + bit[orders[q][u]] * width(u)
        return offset

    def remote(src, dst, send_sem, recv_sem, replica, shard):
        copy = pltpu.make_async_remote_copy(
            src_ref=src, dst_ref=dst, send_sem=send_sem, recv_sem=recv_sem,
            device_id=(replica, shard), device_id_type=MESH,
        )
        copy.start()
        return copy

    def tile(row, offset=0):
        return pl.ds(pl.multiple_of(row + offset, 16), 16)

    def span(offset, column, wide):
        return pl.ds(pl.multiple_of(offset + column, wide), wide)

    sent = []
    local = []

    def chunk_rows(part, shard):
        return aligned((shard * parts + part) * rows, rows)

    def reduced_rows(n):
        return chunk_rows(n // shards, lax.rem(at + 1 + n % shards, shards))

    loads = []
    for n in range(chunks):
        copy = pltpu.make_async_copy(
            grads.at[0, 0, reduced_rows(n), aligned(bit[0] * half, half)], own.at[n], load_sem.at[n]
        )
        copy.start()
        loads.append(copy)

    barrier = pltpu.get_barrier_semaphore()
    for other in partner:
        pl.semaphore_signal(barrier, inc=1, device_id=(other, at), device_id_type=MESH)
    for d in range(1, shards):
        pl.semaphore_signal(barrier, inc=1, device_id=(me, lax.rem(at + d, shards)), device_id_type=MESH)
    pl.semaphore_wait(barrier, len(partner) + shards - 1)

    core = []

    def start_core(n):
        core.append(
            remote(
                grads.at[0, 0, reduced_rows(n), aligned((1 - bit[0]) * half, half)],
                theirs.at[n], core_send.at[n], core_recv.at[n], partner[0], at,
            )
        )
        sent.append(core[n])

    for n in range(2):
        start_core(n)
    states = []

    def load_states():
        for s, (source, target) in enumerate(((master, all_master), (moment_one, all_one), (moment_two, all_two))):
            copy = pltpu.make_async_copy(source, target, state_sem.at[s])
            copy.start()
            states.append(copy)

    halving = {}
    shard_copies = {part: [] for part in range(parts)}

    def start_halving(n, stage, q):
        wide = width(stage)
        b = orders[q][stage]
        if stage == 0:
            source = own.at[n, :, aligned(q * stream + (1 - bit[b]) * wide, wide)]
        else:
            source = summed[stage - 1].at[n, q, :, aligned((1 - bit[b]) * wide, wide)]
        halving[n, stage, q] = remote(
            source, arrived[stage].at[n, q], halve_send.at[n, stage, q], halve_recv.at[n, stage, q], partner[b], at
        )
        sent.append(halving[n, stage, q])

    def reduce(n, step):
        if step == 0:
            loads[n].wait()
            core[n].wait_recv()
            if n + 2 < chunks:
                start_core(n + 2)
            for q in range(2):

                def add(r, c, wide):
                    where = span(q * stream, c, wide)
                    own[n, tile(r), where] = own[n, tile(r), where] + theirs[n, tile(r), where]

                over_tiles(rows, stream, add)
                start_halving(n, 0, q)
            if n == 1:
                load_states()
            return
        stage = step - 1
        for q in range(2):
            halving[n, stage, q].wait_recv()
            kept = bit[orders[q][stage]] * width(stage)

            def add(r, c, wide):
                if stage == 0:
                    mine = own[n, tile(r), span(q * stream + kept, c, wide)]
                else:
                    mine = summed[stage - 1][n, q, tile(r), span(kept, c, wide)]
                summed[stage][n, q, tile(r), pl.ds(c, wide)] = mine + arrived[stage][n, q, tile(r), pl.ds(c, wide)]

            over_tiles(rows, width(stage), add)
            if step < stages:
                start_halving(n, step, q)
        part, i = divmod(n, shards)
        if step == stages and i < shards - 1:
            copy = remote(
                summed[stages - 1].at[n], from_shard.at[part, i], shard_send.at[part, i], shard_recv.at[part, i],
                me, lax.rem(at + 1 + i, shards),
            )
            shard_copies[part].append(copy)
            sent.append(copy)

    piece = width(stages - 1)
    joining = {}
    spread = {}
    pairs = {}
    todo = []

    def join(m, stage, q):
        where = aligned(base(q, stage), width(stage))
        joining[m, stage, q] = remote(
            held.at[m, :, where], held.at[m, :, where], join_send.at[m, stage, q], join_recv.at[m, stage, q],
            partner[orders[q][stage]], at,
        )
        sent.append(joining[m, stage, q])

    def own_piece(part):
        for copy in shard_copies[part]:
            copy.wait_recv()
        m = part * shards
        for q in range(2):
            offset = base(q, stages - 1)

            def finish(r, c, wide):
                total = summed[stages - 1][m + shards - 1, q, tile(r), pl.ds(c, wide)].astype(jnp.float32)
                for i in range(shards - 1):
                    total = total + from_shard[part, i, q, tile(r), pl.ds(c, wide)].astype(jnp.float32)
                held[m, tile(r), span(offset, c, wide)] = total.astype(jnp.bfloat16)

            over_tiles(rows, piece, finish)
            while states:
                states.pop().wait()

            def own_update(r, c, wide):
                total = held[m, tile(r), span(offset, c, wide)].astype(jnp.float32)
                row = tile(r, part * rows)
                where = span(bit[0] * half + offset, c, wide)
                updated, _, _ = adam_update(total, all_master[row, where], all_one[row, where], all_two[row, where])
                own_weights[part, q, tile(r), pl.ds(c, wide)] = updated.astype(jnp.bfloat16)

            over_tiles(rows, piece, own_update)
            for d in range(1, shards):
                spread[part, d, q] = remote(
                    own_weights.at[part, q], held.at[m + d, :, aligned(offset, piece)],
                    spread_send.at[part, d - 1, q], spread_recv.at[part, d - 1, q], me, lax.rem(at + d, shards),
                )
                sent.append(spread[part, d, q])
            join(m, stages - 1, q)

    def update_rows(part, side, group, place):
        start = (bit[0] if side == 0 else 1 - bit[0]) * half
        m = part * shards
        if side == 1 and group == 0:
            pairs[m, place].wait_recv()

        def update(r, c, wide):
            r = pl.ds(group * 16, 16)
            here = span(place * stream, c, wide)
            total = held[m, r, here] if side == 0 else total_pair[part, r, here]
            row = pl.ds(part * rows + group * 16, 16)
            where = span(start + place * stream, c, wide)
            updated, first, second = adam_update(
                total.astype(jnp.float32), all_master[row, where], all_one[row, where], all_two[row, where]
            )
            all_master[row, where] = updated
            all_one[row, where] = first
            all_two[row, where] = second
            row_weights[row, where] = updated.astype(jnp.bfloat16)

        over_tiles(16, stream, update, 1024)
        if group == rows // 16 - 1 and place == 1:
            block = pl.ds(part * rows, rows)
            where = aligned(start, half)
            targets = (
                (all_master, master_out.at[block, where]),
                (all_one, one_out.at[block, where]),
                (all_two, two_out.at[block, where]),
                (row_weights, weights_out.at[chunk_rows(part, at), where]),
            )
            for s, (source, target) in enumerate(targets):
                copy = pltpu.make_async_copy(source.at[block, where], target, out_sem.at[part, side, s])
                copy.start()
                local.append(copy)

    def gather(m, step):
        part, j = divmod(m, shards)
        block = chunk_rows(part, lax.rem(at + shards - j, shards))
        for q in range(2):
            if step > 0:
                joining[m, stages - step, q].wait_recv()
            elif j > 0:
                spread[part, j, q].wait_recv()
            if step < stages:
                if (j, step) != (0, 0):
                    join(m, stages - 1 - step, q)
                continue
            source = held.at[m, :, pl.ds(q * stream, stream)]
            if j == 0:
                target = total_pair.at[part, :, pl.ds(q * stream, stream)]
            else:
                target = weights_out.at[block, aligned(bit[0] * half + q * stream, stream)]
                copy = pltpu.make_async_copy(source, target, store_sem.at[m, q])
                copy.start()
                local.append(copy)
            pairs[m, q] = remote(source, target, pair_send.at[m, q], pair_recv.at[m, q], partner[0], at)
            sent.append(pairs[m, q])
        if step == stages and j == 0:
            todo.extend(
                (part, side, group, place) for side in range(2) for group in range(rows // 16) for place in range(2)
            )

    ahead = 2

    def gather_tick(tick):
        for step in reversed(range(stages + 1)):
            if 0 <= tick - step * ahead < chunks:
                gather(tick - step * ahead, step)
                if todo:
                    update_rows(*todo.pop(0))

    ready = 0
    gathered = 0
    for tick in range(chunks + stages):
        for step in range(stages + 1):
            if 0 <= tick - step < chunks:
                reduce(tick - step, step)
        if tick == (ready + 1) * shards - 1 + stages:
            own_piece(ready)
            ready += 1
        if gathered < ready * shards:
            gather_tick(gathered)
            gathered += 1
    while gathered < chunks + stages * ahead:
        gather_tick(gathered)
        gathered += 1
    while todo:
        update_rows(*todo.pop(0))

    for (m, _), pair in pairs.items():
        if m % shards:
            pair.wait_recv()
    for copy in local:
        copy.wait()
    for copy in sent:
        copy.wait_send()


def write_out(*refs):
    count = len(refs) // 2
    copies = [pltpu.make_async_copy(refs[k], refs[count + k], refs[-1].at[k]) for k in range(count)]
    for copy in copies:
        copy.start()
    for copy in copies:
        copy.wait()


def local(replicas, shards, grads, master, moment_one, moment_two):
    rows, columns = master.shape
    half = columns // 2
    stages = replicas.bit_length() - 2
    piece = half // 2 >> stages
    parts = 2 if rows % 32 == 0 else 1
    chunks = parts * shards
    part = rows // parts
    halves = [(chunks, 2, part, half // 2 >> (t + 1)) for t in range(stages)]
    sem = pltpu.SemaphoreType.DMA
    hbm = pl.BlockSpec(memory_space=pltpu.HBM)
    outs = tuple(
        jax.ShapeDtypeStruct(shape, dtype)
        for shape, dtype in [((rows, columns), jnp.float32)] * 3 + [((rows * shards, columns), jnp.bfloat16)]
    )
    results = pl.pallas_call(
        functools.partial(kernel, replicas, shards, parts),
        out_shape=outs,
        in_specs=[hbm] * 4,
        out_specs=[pl.BlockSpec(memory_space=pl.ANY)] * 4,
        scratch_shapes=[
            pltpu.VMEM((chunks, part, half), jnp.bfloat16),
            pltpu.VMEM((chunks, part, half), jnp.bfloat16),
            pltpu.VMEM((parts, shards - 1, 2, part, piece), jnp.bfloat16),
            pltpu.VMEM((chunks, part, half), jnp.bfloat16),
            pltpu.VMEM((parts, part, half), jnp.bfloat16),
            pltpu.VMEM((parts, 2, part, piece), jnp.bfloat16),
            pltpu.VMEM((rows, columns), jnp.bfloat16),
            *[pltpu.VMEM((rows, columns), jnp.float32)] * 3,
            *[pltpu.VMEM(shape, jnp.bfloat16) for shape in halves * 2],
            sem((chunks,)),
            sem((3,)),
            sem((chunks, 2)),
            sem((parts, 2, 4)),
            *[sem((chunks,))] * 2,
            *[sem((chunks, stages, 2))] * 2,
            *[sem((parts, shards - 1))] * 2,
            *[sem((parts, shards - 1, 2))] * 2,
            *[sem((chunks, stages, 2))] * 2,
            *[sem((chunks, 2))] * 2,
        ],
        compiler_params=pltpu.CompilerParams(
            collective_id=0, has_side_effects=True, vmem_limit_bytes=28 * 1024 * 1024
        ),
        name="reduce_update_gather",
    )(*(pltpu.with_memory_space_constraint(x, pltpu.HBM) for x in (grads, master, moment_one, moment_two)))
    return pl.pallas_call(
        write_out,
        out_shape=outs,
        in_specs=[pl.BlockSpec(memory_space=pltpu.VMEM)] * 4,
        out_specs=[hbm] * 4,
        scratch_shapes=[sem((4,))],
        compiler_params=pltpu.CompilerParams(vmem_limit_bytes=16 * 1024 * 1024),
        name="write_out",
    )(*results)


def solution(mesh):
    placed = (
        P("replica", "shard", None, None),
        P("shard", None),
        P("shard", None),
        P("shard", None),
    )
    return jax.shard_map(
        functools.partial(local, mesh.shape["replica"], mesh.shape["shard"]),
        mesh=mesh,
        in_specs=placed,
        out_specs=(P("shard", None), P("shard", None), P("shard", None), P()),
        check_vma=False,
    )
```
